32 devices in a mesh: dp: 4 (over x, core), blk: 4 (over z), heads: 2 (over y).
Axes of the slice: x: 2, y: 2, z: 4, core: 2. Of those that a mesh axis runs over, the one named last changes fastest.
Arguments:
- hidden_in: bfloat16 [6144, 2048], P(('dp', 'blk')), may hold values from -6 to 6
- memory: bfloat16 [6144, 2048], P(('dp', 'blk')), may hold values from -6 to 6
- lengths: int32 [4, 4], P('dp'), may hold values from 1 to 1344, 1536 in all within a row
- query_weight: bfloat16 [2048, 2048], P(('dp', 'blk'), 'heads'), may hold values from -0.125 to 0.125
- key_weight: bfloat16 [2048, 2048], P(('dp', 'blk'), 'heads'), may hold values from -0.125 to 0.125
- value_weight: bfloat16 [2048, 2048], P(('dp', 'blk'), 'heads'), may hold values from -0.125 to 0.125
- output_weight: bfloat16 [2048, 2048], P(('dp', 'blk'), 'heads'), may hold values from -3 to 3
- gate_weight: bfloat16 [2048, 5504], P(('dp', 'blk'), 'heads'), may hold values from -0.125 to 0.125
- up_weight: bfloat16 [2048, 5504], P(('dp', 'blk'), 'heads'), may hold values from -0.125 to 0.125
- down_weight: bfloat16 [2048, 5504], P(('dp', 'blk'), 'heads'), may hold values from -0.078125 to 0.078125
- attention_gain: bfloat16 [2048], P(('dp', 'blk')), may hold values from 0.099609375 to 1.8984375
- memory_gain: bfloat16 [2048], P(('dp', 'blk')), may hold values from 0.099609375 to 1.8984375
- feedforward_gain: bfloat16 [2048], P(('dp', 'blk')), may hold values from 0.099609375 to 1.8984375
- cotangent: bfloat16 [6144, 2048], P(('dp', 'blk')), may hold values from -6 to 6
Outputs:
- output: bfloat16 [6144, 2048], P(('dp', 'blk'))
- hidden_grad: float32 [6144, 2048], P(('dp', 'blk'))
- memory_grad: float32 [6144, 2048], P(('dp', 'blk'))
- query_weight_grad: float32 [2048, 2048], P(('dp', 'blk'), 'heads')
- key_weight_grad: float32 [2048, 2048], P(('dp', 'blk'), 'heads')
- value_weight_grad: float32 [2048, 2048], P(('dp', 'blk'), 'heads')
- output_weight_grad: float32 [2048, 2048], P(('dp', 'blk'), 'heads')
- gate_weight_grad: float32 [2048, 5504], P(('dp', 'blk'), 'heads')
- up_weight_grad: float32 [2048, 5504], P(('dp', 'blk'), 'heads')
- down_weight_grad: float32 [2048, 5504], P(('dp', 'blk'), 'heads')
- attention_gain_grad: float32 [2048], P(('dp', 'blk'))
- memory_gain_grad: float32 [2048], P(('dp', 'blk'))
- feedforward_gain_grad: float32 [2048], P(('dp', 'blk'))
The draws below stay inside these ranges and needn't reach their ends.
Inputs may be any that keep to these rules, and one draw needn't show every extreme that they name: Each row of lengths sums to 1536, and its largest entry is exactly 1344.
All inputs are finite; a program needn't handle non-finite values.
Results may differ from the reference program's by a relative error of at most 0.02.
Values may be sent and summed in bfloat16 or wider, within the bound.
A program may use at most 384 MiB of HBM per device.

```python
import math
import jax
import jax.numpy as jnp
import numpy as np
from jax import lax

D = 2048
HEADS = 16
HEAD = 128
FF = 5504
SEQS = 4
HD = 2048
GROUPS = 4
GROUP_TOK = 1536
TOKENS = 6144
LONGEST = 1344


def steps_of(own_key, extent, cuts, least, high):
    def one(axis_at, blocks):
        steps = jax.random.uniform(jax.random.fold_in(jax.random.fold_in(own_key, 6), axis_at), (blocks,), jnp.float32, least / len(cuts), high / len(cuts))
        return jnp.repeat(jnp.exp(steps), extent[axis_at] // blocks).reshape((-1,) + (1,) * (len(extent) - axis_at - 1))

    level = one(*cuts[0])
    for cut in cuts[1:]:
        level = level * one(*cut)
    return level


def profile(number_of, total, limit, lean):
    weights = [(1 << 20) // math.isqrt(rank ** lean) + 1 for rank in range(2, number_of + 1)]
    rest, given = total - limit - (number_of - 1), [1] * (number_of - 1)
    while rest > 0:
        movable = [i for i in range(number_of - 1) if given[i] < limit]
        mass, left = sum([weights[i] for i in movable]), rest
        for i in movable:
            addition = min(limit - given[i], max(1, left * weights[i] // mass), rest)
            given[i] = given[i] + addition
            rest = rest - addition
    return np.array([limit] + given)


def ragged(own_key, count, total, bound, lean):
    if count == 2:
        one = jax.random.randint(own_key, (), max(1, total - bound), min(bound, total - 1) + 1)
        return jnp.stack([one, total - one])
    sizes = jnp.asarray(profile(count, total, bound, lean), jnp.int32)
    twos = (count - 1) // 2
    giver, sink = sizes[1:1 + 2 * twos:2], sizes[2:2 + 2 * twos:2]
    room = jnp.minimum(giver - 1, bound - sink)
    moved = jax.random.randint(jax.random.fold_in(own_key, 1), (twos,), 0, 1 << 20) % (room + 1)
    sizes = sizes.at[1:1 + 2 * twos:2].set(giver - moved).at[2:2 + 2 * twos:2].set(sink + moved)
    return sizes[jax.random.permutation(jax.random.fold_in(own_key, 2), count)]


def normal_values(key, shape, scale, most, shards=(), kind=jnp.bfloat16):
    level = steps_of(key, shape, shards, -0.22, 0.18) if shards else 1.0
    array = jax.random.normal(key, shape, jnp.float32) * scale * level
    return jnp.minimum(jnp.maximum(array, -most), most).astype(kind)


def setup_inputs(seed: int = 0) -> dict:
    seeds = jax.random.split(jax.random.key(seed), 15)
    return {
        "hidden_in": normal_values(seeds[0], (TOKENS, D), 1.0, 6.0, ((0, 16),)),
        "memory": normal_values(seeds[1], (TOKENS, D), 1.0, 6.0, ((0, 16),)),
        "lengths": jax.vmap(lambda own: ragged(own, SEQS, GROUP_TOK, LONGEST, 2))(jax.random.split(seeds[2], GROUPS)).reshape((GROUPS, SEQS)).astype(jnp.int32),
        "query_weight": normal_values(seeds[3], (D, HD), D ** -0.5, 0.125, ((0, 16), (1, 2))),
        "key_weight": normal_values(seeds[4], (D, HD), D ** -0.5, 0.125, ((0, 16), (1, 2))),
        "value_weight": normal_values(seeds[5], (D, HD), D ** -0.5, 0.125, ((0, 16), (1, 2))),
        "output_weight": normal_values(seeds[6], (D, HD), (max(HD // 512, 1)) ** -0.5, 3.0, ((0, 16), (1, 2))),
        "gate_weight": normal_values(seeds[7], (D, FF), D ** -0.5, 0.125, ((0, 16), (1, 2))),
        "up_weight": normal_values(seeds[8], (D, FF), D ** -0.5, 0.125, ((0, 16), (1, 2))),
        "down_weight": normal_values(seeds[9], (D, FF), FF ** -0.5, 0.078125, ((0, 16), (1, 2))),
        "attention_gain": jnp.clip(1.0 + 0.18 * jax.random.normal(seeds[10], (D,), jnp.float32), 0.099609375, 1.8984375).astype(jnp.bfloat16),
        "memory_gain": jnp.clip(1.0 + 0.18 * jax.random.normal(seeds[11], (D,), jnp.float32), 0.099609375, 1.8984375).astype(jnp.bfloat16),
        "feedforward_gain": jnp.clip(1.0 + 0.18 * jax.random.normal(seeds[12], (D,), jnp.float32), 0.099609375, 1.8984375).astype(jnp.bfloat16),
        "cotangent": normal_values(seeds[13], (TOKENS, D), 1.0, 6.0, ((0, 16),)),
    }


EPSILON = 1e-06
NEGATIVE = -1e+30

@jax.custom_vjp
def low(v):
    return lax.optimization_barrier(v.astype(jnp.bfloat16)).astype(jnp.float32)

@jax.custom_vjp
def low_back(v):
    return v

def low_keep(v):
    return (low(v), None)

def low_pass(kept, grad):
    return (grad,)

def back_keep(v):
    return (v, None)

def back_low(kept, grad):
    return (low(grad),)
low.defvjp(low_keep, low_pass)
low_back.defvjp(back_keep, back_low)

def round_both(values):
    return low(low_back(values))

def rms_scale(values, gain):
    return values * lax.rsqrt(lax.optimization_barrier(jnp.mean(values * values, axis=-1, keepdims=True)) + EPSILON) * gain

def matmul(left, right):
    return jnp.dot(left, right, precision=lax.Precision.HIGHEST)

def matmul_rows(left, right):
    return lax.dot_general(left, right, (((1,), (1,)), ((), ())), precision=lax.Precision.HIGHEST)

def attend_block(query_block, key_group, value_group, query_pos, query_doc, key_doc):
    factor = 1.0 / math.sqrt(HEAD)
    scores = jnp.einsum('qhd,khd->hqk', query_block, key_group, precision=lax.Precision.HIGHEST) * factor
    scores = low_back(scores)
    key_pos = jnp.arange(key_group.shape[0], dtype=jnp.int32)
    allowed = (key_pos[None, :] <= query_pos[:, None]) & (key_doc[None, :] == query_doc[:, None])
    scores = jnp.where(allowed[None], scores, NEGATIVE)
    highest = lax.optimization_barrier(jnp.max(scores, axis=-1, keepdims=True))
    weights = jnp.exp(scores - highest)
    probs = weights / lax.optimization_barrier(jnp.sum(weights, axis=-1, keepdims=True))
    return jnp.einsum('hqk,khd->qhd', low(probs), value_group, precision=lax.Precision.HIGHEST)

def attention(queries, keys, values, documents):
    block_rows = min(512, GROUP_TOK)
    block_count = GROUP_TOK // block_rows
    query_all = queries.reshape(GROUPS, block_count, block_rows, HEADS, HEAD)
    key_all = keys.reshape(GROUPS, GROUP_TOK, HEADS, HEAD)
    value_all = values.reshape(GROUPS, GROUP_TOK, HEADS, HEAD)

    def one_group(group_items):
        query_group, key_group, value_group, doc_group = group_items

        def one_block(block_items):
            query_block, number = block_items
            begin = number * block_rows
            query_pos = begin + jnp.arange(block_rows, dtype=jnp.int32)
            query_doc = lax.dynamic_slice_in_dim(doc_group, begin, block_rows)
            return attend_block(query_block, key_group, value_group, query_pos, query_doc, doc_group)
        return lax.map(jax.checkpoint(one_block), (query_group, jnp.arange(block_count, dtype=jnp.int32)))
    result = lax.map(one_group, (query_all, key_all, value_all, documents))
    return result.reshape(TOKENS, HEADS * HEAD)

def forward(hidden, memory, query_weight, key_weight, value_weight, output_weight, gate_weight, up_weight, down_weight, attention_gain, memory_gain, feedforward_gain, documents):
    memory_in = low(rms_scale(memory, memory_gain))
    keys = round_both(matmul(memory_in, key_weight))
    values = round_both(matmul(memory_in, value_weight))
    normed_in = low(rms_scale(hidden, attention_gain))
    queries = round_both(matmul(normed_in, query_weight))
    head_shape = (TOKENS, HEADS, HEAD)
    context = round_both(attention(queries.reshape(head_shape), keys.reshape(head_shape), values.reshape(head_shape), documents))
    attended = hidden + low_back(matmul_rows(context, output_weight))
    normed_mid = low(rms_scale(attended, feedforward_gain))
    gate = low_back(matmul(normed_mid, gate_weight))
    upward = low_back(matmul(normed_mid, up_weight))
    activation = low(jax.nn.silu(gate) * upward)
    return attended + low_back(matmul_rows(activation, down_weight))

def reference(hidden_in, memory, lengths, query_weight, key_weight, value_weight, output_weight, gate_weight, up_weight, down_weight, attention_gain, memory_gain, feedforward_gain, cotangent):
    doc_ends = jnp.cumsum(lengths, axis=1, dtype=jnp.int32)
    positions = jnp.arange(GROUP_TOK, dtype=jnp.int32)
    documents = lax.optimization_barrier(jnp.sum((positions[None, :, None] >= doc_ends[:, None, :]).astype(jnp.int32), axis=2)).astype(jnp.int32)
    floats = (hidden_in.astype(jnp.float32), memory.astype(jnp.float32), query_weight.astype(jnp.float32), key_weight.astype(jnp.float32), value_weight.astype(jnp.float32), output_weight.astype(jnp.float32), gate_weight.astype(jnp.float32), up_weight.astype(jnp.float32), down_weight.astype(jnp.float32), attention_gain.astype(jnp.float32), memory_gain.astype(jnp.float32), feedforward_gain.astype(jnp.float32))

    def wrapped(*arrays):
        return forward(*arrays, documents)
    result, pullback = jax.vjp(wrapped, *floats)
    grads = pullback(cotangent.astype(jnp.float32))
    return (result.astype(jnp.bfloat16), grads[0], grads[1], grads[2], grads[3], grads[4], grads[5], grads[6], grads[7], grads[8], grads[9], grads[10], grads[11])
```

```python
import math

import jax
import jax.numpy as jnp
from jax import lax
from jax.sharding import PartitionSpec as P

HEAD = 128
LANES = 128
EPSILON = 1e-06
NEGATIVE = -1e30


def rms_scale(values, gain):
    return values * lax.rsqrt(jnp.mean(values * values, axis=-1, keepdims=True) + EPSILON) * gain


def plain_dot(left, right):
    return jnp.dot(left, right, preferred_element_type=jnp.float32)


def dot_rows(left, right):
    return lax.dot_general(
        left, right, (((1,), (1,)), ((), ())), preferred_element_type=jnp.float32
    )


def dot_cols(left, right):
    return lax.dot_general(
        left, right, (((0,), (0,)), ((), ())), preferred_element_type=jnp.float32
    )


def doc_number(positions, doc_ends):
    return jnp.sum((positions[:, None] >= doc_ends[None, :]).astype(jnp.int32), axis=1)


def swap(array, axis, bit):
    size = lax.axis_size(axis)
    return lax.ppermute(array, axis, [(i, i ^ bit) for i in range(size)])


def pair_sum(part):
    low = part.astype(jnp.bfloat16)
    if lax.axis_size("heads") != 2:
        return lax.psum(low, "heads").astype(jnp.float32)
    other = swap(low, "heads", 1)
    return low.astype(jnp.float32) + other.astype(jnp.float32)


def fold_steps():
    steps = []
    for axis in ("dp", "blk"):
        size, bit = lax.axis_size(axis), 1
        while bit < size:
            steps.append((axis, bit))
            bit *= 2
    return steps


def fold_order(width):
    steps = fold_steps()
    shards = 2 ** len(steps)
    part = width // shards
    here = {axis: lax.axis_index(axis) for axis in ("dp", "blk")}
    offsets = []
    for place in range(shards):
        flip = {"dp": 0, "blk": 0}
        for number, (axis, bit) in enumerate(steps):
            if place >> (len(steps) - 1 - number) & 1:
                flip[axis] |= bit
        shard = (here["dp"] ^ flip["dp"]) * lax.axis_size("blk") + (here["blk"] ^ flip["blk"])
        offsets.append(shard * part)
    return offsets, part


def fold_columns(array):
    offsets, part = fold_order(array.shape[1])
    return jnp.concatenate(
        [lax.dynamic_slice_in_dim(array, offset, part, axis=1) for offset in offsets], axis=1
    )


def fold_product(left, right, kind=jnp.bfloat16):
    steps = fold_steps()
    size = left.shape[1]
    pieces = []
    for _ in steps:
        size //= 2
        pieces.append((size, 2 * size))
    pieces.append((0, size))
    arrived = []
    for (axis, bit), (low, high) in zip(steps, pieces):
        part = dot_cols(left[:, low:high], right)
        for earlier in arrived:
            part = part + earlier[low:high].astype(jnp.float32)
        arrived.append(swap(part.astype(kind), axis, bit))
    low, high = pieces[-1]
    part = dot_cols(left[:, low:high], right)
    for earlier in arrived:
        part = part + earlier[low:high].astype(jnp.float32)
    return part


def fold_vector(vector):
    offsets, part = fold_order(vector.shape[-1])
    held = jnp.stack(
        [lax.dynamic_slice_in_dim(vector, offset, part, axis=-1) for offset in offsets], axis=0
    )
    for axis, bit in fold_steps():
        half = held.shape[0] // 2
        held = held[:half] + swap(held[half:], axis, bit)
    return held[0]


def to_heads(pieces, blocks):
    rows, width = pieces[0].shape
    part = width // blocks
    packed = jnp.stack(
        [
            jnp.concatenate([piece[:, i * part : (i + 1) * part] for piece in pieces], axis=1)
            for i in range(blocks)
        ],
        axis=0,
    )
    moved = lax.all_to_all(packed, "blk", 0, 0)
    flat = moved.reshape(rows * blocks, part * len(pieces))
    return [flat[:, i * part : (i + 1) * part] for i in range(len(pieces))]


def to_blocks(pieces, blocks):
    length, part = pieces[0].shape
    rows = length // blocks
    packed = jnp.concatenate(pieces, axis=1).reshape(blocks, rows, part * len(pieces))
    moved = lax.all_to_all(packed, "blk", 0, 0)
    return [
        jnp.concatenate([moved[j, :, i * part : (i + 1) * part] for j in range(blocks)], axis=1)
        for i in range(len(pieces))
    ]


def local(
    hidden_in,
    memory,
    lengths,
    query_weight,
    key_weight,
    value_weight,
    output_weight,
    gate_weight,
    up_weight,
    down_weight,
    attention_gain,
    memory_gain,
    feedforward_gain,
    cotangent,
):
    rows, features = hidden_in.shape
    blocks = lax.axis_size("blk")
    width = query_weight.shape[1]
    hidden_units = gate_weight.shape[1]
    heads_local = width // HEAD
    factor = 1.0 / math.sqrt(HEAD)
    spread = heads_local % blocks == 0
    doc_ends = jnp.cumsum(lengths[0], dtype=jnp.int32)

    gains = jnp.stack([attention_gain, memory_gain, feedforward_gain], axis=1)
    gains = jnp.pad(gains, ((0, 0), (0, LANES - gains.shape[1])))
    attn_mine = jnp.concatenate(
        [query_weight, key_weight, value_weight, output_weight, gains], axis=1
    )
    attn_full = lax.all_gather(attn_mine, ("dp", "blk"), axis=0, tiled=True)
    cuts = 2
    chunk = -(-hidden_units // (cuts * LANES)) * LANES
    spans = [(i * chunk, min(hidden_units, (i + 1) * chunk)) for i in range(cuts)]
    ffn_mine = []
    for start, stop in spans:
        for weight in (gate_weight, up_weight, down_weight):
            ffn_mine.append(
                jnp.pad(weight[:, start:stop], ((0, 0), (0, chunk - (stop - start))))
            )
    ffn_mine = jnp.concatenate(ffn_mine, axis=1)
    ffn_mine, attn_full = lax.optimization_barrier((ffn_mine, attn_full))
    ffn_full = lax.all_gather(ffn_mine, ("dp", "blk"), axis=0, tiled=True)

    full_query = attn_full[:, :width]
    full_key = attn_full[:, width : 2 * width]
    full_value = attn_full[:, 2 * width : 3 * width]
    full_output = attn_full[:, 3 * width : 4 * width]
    full_gains = attn_full[:, 4 * width : 4 * width + 3].astype(jnp.float32).T
    input_gain, source_gain, mid_gain = full_gains[0], full_gains[1], full_gains[2]

    hidden_float = hidden_in.astype(jnp.float32)
    memory_float = memory.astype(jnp.float32)
    memory_low = rms_scale(memory_float, source_gain).astype(jnp.bfloat16)
    normed_low = rms_scale(hidden_float, input_gain).astype(jnp.bfloat16)
    key_low = plain_dot(memory_low, full_key).astype(jnp.bfloat16)
    value_low = plain_dot(memory_low, full_value).astype(jnp.bfloat16)
    query_low = plain_dot(normed_low, full_query).astype(jnp.bfloat16)

    length = rows * blocks
    key_pos = jnp.arange(length, dtype=jnp.int32)
    key_doc = doc_number(key_pos, doc_ends)
    if spread:
        query_all, key_all, value_all = to_heads([query_low, key_low, value_low], blocks)
        query_pos = key_pos
    else:
        query_all = query_low
        key_all = lax.all_gather(key_low, "blk", axis=0, tiled=True)
        value_all = lax.all_gather(value_low, "blk", axis=0, tiled=True)
        query_pos = lax.axis_index("blk") * rows + jnp.arange(rows, dtype=jnp.int32)
    query_doc = doc_number(query_pos, doc_ends)
    allowed = (key_pos[None, :] <= query_pos[:, None]) & (key_doc[None, :] == query_doc[:, None])
    query_heads = query_all.reshape(query_all.shape[0], -1, HEAD)
    key_heads = key_all.reshape(length, -1, HEAD)
    value_heads = value_all.reshape(length, -1, HEAD)

    def scores_of():
        return (
            jnp.einsum("qhd,khd->hqk", query_heads, key_heads, preferred_element_type=jnp.float32)
            * factor
        )

    masked = jnp.where(allowed[None], scores_of(), NEGATIVE)
    top = jnp.max(masked, axis=-1)
    weights = jnp.where(allowed[None], jnp.exp(masked - top[..., None]), 0.0)
    total = jnp.sum(weights, axis=-1)
    added = jnp.einsum(
        "hqk,khd->qhd", weights.astype(jnp.bfloat16), value_heads, preferred_element_type=jnp.float32
    )
    context = added / total.T[:, :, None]
    log_total = top + jnp.log(total)
    context_all = context.reshape(context.shape[0], -1).astype(jnp.bfloat16)
    context_low = to_blocks([context_all], blocks)[0] if spread else context_all

    attended = hidden_float + pair_sum(dot_rows(context_low, full_output))
    mid_low = rms_scale(attended, mid_gain).astype(jnp.bfloat16)

    mid_fold = fold_columns(mid_low)
    cot_fold = fold_columns(cotangent)
    cot_float = cotangent.astype(jnp.float32)
    ffn_part, mid_part = 0.0, 0.0
    ffn_shares = ([], [], [])
    for number, (start, stop) in enumerate(spans):
        own = ffn_full[:, 3 * chunk * number : 3 * chunk * (number + 1)]
        span_gate, span_up, span_down = own[:, :chunk], own[:, chunk : 2 * chunk], own[:, 2 * chunk :]
        gate = plain_dot(mid_low, span_gate)
        upward = plain_dot(mid_low, span_up)
        sigma = jax.nn.sigmoid(gate)
        silu_gate = gate * sigma
        act_low = (silu_gate * upward).astype(jnp.bfloat16)
        act_grad = plain_dot(cotangent, span_down)
        gate_grad_low = (act_grad * upward * sigma * (1.0 + gate * (1.0 - sigma))).astype(
            jnp.bfloat16
        )
        up_grad_low = (act_grad * silu_gate).astype(jnp.bfloat16)
        mid_part = mid_part + dot_rows(gate_grad_low, span_gate) + dot_rows(up_grad_low, span_up)
        ffn_part = ffn_part + dot_rows(act_low, span_down)
        size = stop - start
        ffn_shares[0].append(fold_product(mid_fold, gate_grad_low[:, :size]))
        ffn_shares[1].append(fold_product(mid_fold, up_grad_low[:, :size]))
        ffn_shares[2].append(fold_product(cot_fold, act_low[:, :size]))
    gate_share, up_share, down_share = (jnp.concatenate(parts, axis=1) for parts in ffn_shares)
    mid_grad = pair_sum(mid_part)
    output = (attended + pair_sum(ffn_part)).astype(jnp.bfloat16)
    attended_norm_grad, mid_gain_grad = jax.vjp(rms_scale, attended, mid_gain)[1](mid_grad)
    attended_grad = cot_float + attended_norm_grad

    resid_low = attended_grad.astype(jnp.bfloat16)
    output_share = fold_product(fold_columns(resid_low), context_low)
    context_grad_low = plain_dot(resid_low, full_output).astype(jnp.bfloat16)
    if spread:
        context_grad_all = to_heads([context_grad_low], blocks)[0]
    else:
        context_grad_all = context_grad_low
    context_grad_heads = context_grad_all.reshape(context_grad_all.shape[0], -1, HEAD)
    delta = jnp.sum(context_grad_heads.astype(jnp.float32) * context, axis=-1).T
    probs = jnp.where(allowed[None], jnp.exp(scores_of() - log_total[..., None]), 0.0)
    probs_low = probs.astype(jnp.bfloat16)
    prob_grad = jnp.einsum(
        "qhd,khd->hqk", context_grad_heads, value_heads, preferred_element_type=jnp.float32
    )
    score_grad = (probs * (prob_grad - delta[..., None])).astype(jnp.bfloat16)
    query_grad = (
        jnp.einsum("hqk,khd->qhd", score_grad, key_heads, preferred_element_type=jnp.float32)
        * factor
    )
    key_grad = (
        jnp.einsum("hqk,qhd->khd", score_grad, query_heads, preferred_element_type=jnp.float32)
        * factor
    )
    value_grad = jnp.einsum(
        "hqk,qhd->khd", probs_low, context_grad_heads, preferred_element_type=jnp.float32
    )
    query_grad, key_grad, value_grad = (
        grad.reshape(grad.shape[0], -1).astype(jnp.bfloat16)
        for grad in (query_grad, key_grad, value_grad)
    )
    if spread:
        query_grad_low, key_grad_low, value_grad_low = to_blocks(
            [query_grad, key_grad, value_grad], blocks
        )
    else:
        query_grad_low = query_grad
        mine = lax.psum_scatter(
            jnp.concatenate([key_grad, value_grad], axis=1), "blk", scatter_dimension=0, tiled=True
        )
        key_grad_low, value_grad_low = mine[:, :width], mine[:, width:]

    normed_grad = pair_sum(dot_rows(query_grad_low, full_query))
    memory_in_grad = pair_sum(
        dot_rows(key_grad_low, full_key) + dot_rows(value_grad_low, full_value)
    )
    normed_fold, memory_fold = fold_columns(normed_low), fold_columns(memory_low)
    query_share = fold_product(normed_fold, query_grad_low)
    key_share = fold_product(memory_fold, key_grad_low)
    value_share = fold_product(memory_fold, value_grad_low)
    hidden_norm_grad, input_gain_grad = jax.vjp(rms_scale, hidden_float, input_gain)[1](normed_grad)
    memory_grad, source_gain_grad = jax.vjp(rms_scale, memory_float, source_gain)[1](memory_in_grad)
    hidden_grad = attended_grad + hidden_norm_grad
    gain_shares = fold_vector(jnp.stack([input_gain_grad, source_gain_grad, mid_gain_grad], axis=0))
    return (
        output,
        hidden_grad,
        memory_grad,
        query_share,
        key_share,
        value_share,
        output_share,
        gate_share,
        up_share,
        down_share,
        gain_shares[0],
        gain_shares[1],
        gain_shares[2],
    )


def solution(mesh):
    tokens = P(("dp", "blk"), None)
    weight = P(("dp", "blk"), "heads")
    gain = P(("dp", "blk"))
    return jax.shard_map(
        local,
        mesh=mesh,
        in_specs=(tokens, tokens, P("dp", None)) + (weight,) * 7 + (gain,) * 3 + (tokens,),
        out_specs=(tokens,) * 3 + (weight,) * 7 + (gain,) * 3,
        check_vma=False,
    )
```

```python
import functools
import math

import jax
import jax.numpy as jnp
from jax import lax
from jax.experimental import pallas as pl
from jax.experimental.pallas import tpu as pltpu
from jax.sharding import PartitionSpec as P

MESH = pl.DeviceIdType.MESH
HEAD = 128
LANES = 128
EPSILON = 1e-06
NEGATIVE = -1e30


def rms_scale(values, gain):
    return values * lax.rsqrt(jnp.mean(values * values, axis=-1, keepdims=True) + EPSILON) * gain


def plain_dot(left, right):
    return jnp.dot(left, right, preferred_element_type=jnp.float32)


def dot_rows(left, right):
    return lax.dot_general(
        left, right, (((1,), (1,)), ((), ())), preferred_element_type=jnp.float32
    )


def dot_cols(left, right):
    return lax.dot_general(
        left, right, (((0,), (0,)), ((), ())), preferred_element_type=jnp.float32
    )


def doc_number(positions, doc_ends):
    return jnp.sum((positions[:, None] >= doc_ends[None, :]).astype(jnp.int32), axis=1)


def swap(array, axis, bit):
    size = lax.axis_size(axis)
    return lax.ppermute(array, axis, [(i, i ^ bit) for i in range(size)])


def pair_sum(part):
    low = part.astype(jnp.bfloat16)
    if lax.axis_size("heads") != 2:
        return lax.psum(low, "heads").astype(jnp.float32)
    other = swap(low, "heads", 1)
    return low.astype(jnp.float32) + other.astype(jnp.float32)


def fold_steps():
    steps = []
    for axis in ("dp", "blk"):
        size, bit = lax.axis_size(axis), 1
        while bit < size:
            steps.append((axis, bit))
            bit *= 2
    return steps


def fold_order(width):
    steps = fold_steps()
    shards = 2 ** len(steps)
    part = width // shards
    offsets = []
    for place in range(shards):
        at = {axis: lax.axis_index(axis) for axis in ("dp", "blk")}
        for number, (axis, bit) in enumerate(steps):
            if place >> (len(steps) - 1 - number) & 1:
                at[axis] = flipped(at[axis], bit)
        offsets.append((at["dp"] * lax.axis_size("blk") + at["blk"]) * part)
    return offsets, part


def flipped(index, bit):
    return index + bit * (1 - 2 * ((index // bit) % 2))


def fold_kernel(steps, edges, tiles, width, slots, left_ref, right_ref, out_ref, *scratch):
    count = len(steps)
    held, load_sem, send_sem, recv_sem, credit = scratch[:5]
    sent, got = scratch[5 : 5 + count], scratch[5 + count :]
    lefts, features = held.shape[:2]
    mesh_axes = ("dp", "blk", "heads")
    here = {axis: lax.axis_index(axis) for axis in mesh_axes}
    partners = []
    for axis, bit in steps:
        partners.append(
            tuple(flipped(here[a], bit) if a == axis else here[a] for a in mesh_axes)
        )
    offsets, part = fold_order(features)
    loads = []
    for number in range(lefts):
        for place, offset in enumerate(offsets):
            loads.append(
                pltpu.make_async_copy(
                    left_ref.at[number, pl.ds(pl.multiple_of(offset, part), part)],
                    held.at[number, pl.ds(place * part, part)],
                    load_sem.at[number, place],
                )
            )
    for load in loads:
        load.start()
    barrier = pltpu.get_barrier_semaphore()
    for partner in partners:
        pl.semaphore_signal(barrier, inc=1, device_id=partner, device_id_type=MESH)
    pl.semaphore_wait(barrier, count)
    for load in loads:
        load.wait()

    def transfer(step, tile):
        return pltpu.make_async_remote_copy(
            src_ref=sent[step].at[lax.rem(tile, 2)],
            dst_ref=got[step].at[lax.rem(tile, slots)],
            send_sem=send_sem.at[step, lax.rem(tile, 2)],
            recv_sem=recv_sem.at[step, lax.rem(tile, slots)],
            device_id=partners[step],
            device_id_type=MESH,
        )

    def stage(number, tile):
        slot = lax.rem(tile, slots)
        if number > 0:
            transfer(number - 1, tile).wait_recv()
        last = number == count
        low = 0 if last else features >> (number + 1)
        high = features >> number
        group = jnp.int32(0)
        for edge in edges:
            group = group + (tile >= edge).astype(jnp.int32)
        columns = pl.ds(pl.multiple_of(tile * width, width), width)
        total = jnp.dot(
            held[group, low:high], right_ref[:, columns], preferred_element_type=jnp.float32
        )
        for earlier in range(number):
            total = total + got[earlier][slot, low:high].astype(jnp.float32)
        if last:
            out_ref[:, columns] = total

            @pl.when(tile < tiles - slots)
            def _():
                for step, partner in enumerate(partners):
                    pl.semaphore_signal(
                        credit.at[step], inc=1, device_id=partner, device_id_type=MESH
                    )

            return

        @pl.when(tile >= 2)
        def _():
            transfer(number, tile).wait_send()

        sent[number][lax.rem(tile, 2)] = total.astype(jnp.bfloat16)

        @pl.when(tile >= slots)
        def _():
            pl.semaphore_wait(credit.at[number], 1)

        transfer(number, tile).start()

    def turn(index, carry):
        for number in range(count + 1):
            tile = index - number

            @pl.when((tile >= 0) & (tile < tiles))
            def _(number=number, tile=tile):
                stage(number, tile)

        return carry

    lax.fori_loop(0, tiles + count, turn, 0)
    for step in range(count):
        for tile in range(max(0, tiles - 2), tiles):
            transfer(step, jnp.int32(tile)).wait_send()


def fold_products(groups, call, width=128, slots=8):
    steps = fold_steps()
    count = len(steps)
    lefts = jnp.stack([left.T for left, _ in groups], axis=0)
    rights = jnp.concatenate([right for _, many in groups for right in many], axis=1)
    edges, tiles = [], 0
    for _, many in groups:
        tiles += sum(right.shape[1] for right in many) // width
        edges.append(tiles)
    slots = min(slots, tiles)
    number, features, rows = lefts.shape
    sizes = [features >> (step + 1) for step in range(count)]
    buffers = [pltpu.VMEM((2, size, width), jnp.bfloat16) for size in sizes]
    buffers += [pltpu.VMEM((slots, size, width), jnp.bfloat16) for size in sizes]
    folded = pl.pallas_call(
        functools.partial(fold_kernel, steps, edges[:-1], tiles, width, slots),
        out_shape=jax.ShapeDtypeStruct((features >> count, tiles * width), jnp.float32),
        in_specs=[
            pl.BlockSpec(memory_space=pl.ANY),
            pl.BlockSpec(memory_space=pltpu.VMEM),
        ],
        out_specs=pl.BlockSpec(memory_space=pltpu.VMEM),
        scratch_shapes=[
            pltpu.VMEM((number, features, rows), jnp.bfloat16),
            pltpu.SemaphoreType.DMA((number, 1 << count)),
            pltpu.SemaphoreType.DMA((count, 2)),
            pltpu.SemaphoreType.DMA((count, slots)),
            pltpu.SemaphoreType.REGULAR((count,)),
            *buffers,
        ],
        compiler_params=pltpu.CompilerParams(
            collective_id=call, has_side_effects=True, vmem_limit_bytes=60 * 1024 * 1024
        ),
        cost_estimate=pl.CostEstimate(
            flops=2 * features * rows * tiles * width,
            bytes_accessed=tiles * width * features * 8,
            transcendentals=0,
        ),
    )(lefts, rights)
    shares, at = [], 0
    for _, many in groups:
        shares.append([])
        for right in many:
            shares[-1].append(folded[:, at : at + right.shape[1]])
            at += right.shape[1]
    return shares


def fold_vector(vector):
    offsets, part = fold_order(vector.shape[-1])
    held = jnp.stack(
        [lax.dynamic_slice_in_dim(vector, offset, part, axis=-1) for offset in offsets], axis=0
    )
    for axis, bit in fold_steps():
        half = held.shape[0] // 2
        held = held[:half] + swap(held[half:], axis, bit)
    return held[0]


def to_heads(pieces, blocks):
    rows, width = pieces[0].shape
    part = width // blocks
    packed = jnp.stack(
        [
            jnp.concatenate([piece[:, i * part : (i + 1) * part] for piece in pieces], axis=1)
            for i in range(blocks)
        ],
        axis=0,
    )
    moved = lax.all_to_all(packed, "blk", 0, 0)
    flat = moved.reshape(rows * blocks, part * len(pieces))
    return [flat[:, i * part : (i + 1) * part] for i in range(len(pieces))]


def to_blocks(pieces, blocks):
    length, part = pieces[0].shape
    rows = length // blocks
    packed = jnp.concatenate(pieces, axis=1).reshape(blocks, rows, part * len(pieces))
    moved = lax.all_to_all(packed, "blk", 0, 0)
    return [
        jnp.concatenate([moved[j, :, i * part : (i + 1) * part] for j in range(blocks)], axis=1)
        for i in range(len(pieces))
    ]


def local(
    hidden_in,
    memory,
    lengths,
    query_weight,
    key_weight,
    value_weight,
    output_weight,
    gate_weight,
    up_weight,
    down_weight,
    attention_gain,
    memory_gain,
    feedforward_gain,
    cotangent,
):
    rows, features = hidden_in.shape
    blocks = lax.axis_size("blk")
    width = query_weight.shape[1]
    hidden_units = gate_weight.shape[1]
    heads_local = width // HEAD
    factor = 1.0 / math.sqrt(HEAD)
    spread = heads_local % blocks == 0
    doc_ends = jnp.cumsum(lengths[0], dtype=jnp.int32)

    gains = jnp.stack([attention_gain, memory_gain, feedforward_gain], axis=1)
    gains = jnp.pad(gains, ((0, 0), (0, LANES - gains.shape[1])))
    attn_mine = jnp.concatenate(
        [query_weight, key_weight, value_weight, output_weight, gains], axis=1
    )
    attn_full = lax.all_gather(attn_mine, ("dp", "blk"), axis=0, tiled=True)
    padded = -(-hidden_units // (2 * LANES)) * (2 * LANES)
    ffn_mine = [
        jnp.pad(weight, ((0, 0), (0, padded - hidden_units)))
        for weight in (gate_weight, up_weight, down_weight)
    ]
    ffn_mine = jnp.concatenate(ffn_mine, axis=1)
    ffn_mine, attn_full = lax.optimization_barrier((ffn_mine, attn_full))
    ffn_full = lax.all_gather(ffn_mine, ("dp", "blk"), axis=0, tiled=True)

    full_query = attn_full[:, :width]
    full_key = attn_full[:, width : 2 * width]
    full_value = attn_full[:, 2 * width : 3 * width]
    full_output = attn_full[:, 3 * width : 4 * width]
    full_gains = attn_full[:, 4 * width : 4 * width + 3].astype(jnp.float32).T
    input_gain, source_gain, mid_gain = full_gains[0], full_gains[1], full_gains[2]

    hidden_float = hidden_in.astype(jnp.float32)
    memory_float = memory.astype(jnp.float32)
    memory_low = rms_scale(memory_float, source_gain).astype(jnp.bfloat16)
    normed_low = rms_scale(hidden_float, input_gain).astype(jnp.bfloat16)
    key_low = plain_dot(memory_low, full_key).astype(jnp.bfloat16)
    value_low = plain_dot(memory_low, full_value).astype(jnp.bfloat16)
    query_low = plain_dot(normed_low, full_query).astype(jnp.bfloat16)

    length = rows * blocks
    key_pos = jnp.arange(length, dtype=jnp.int32)
    key_doc = doc_number(key_pos, doc_ends)
    if spread:
        query_all, key_all, value_all = to_heads([query_low, key_low, value_low], blocks)
        query_pos = key_pos
    else:
        query_all = query_low
        key_all = lax.all_gather(key_low, "blk", axis=0, tiled=True)
        value_all = lax.all_gather(value_low, "blk", axis=0, tiled=True)
        query_pos = lax.axis_index("blk") * rows + jnp.arange(rows, dtype=jnp.int32)
    query_doc = doc_number(query_pos, doc_ends)
    allowed = (key_pos[None, :] <= query_pos[:, None]) & (key_doc[None, :] == query_doc[:, None])
    query_heads = query_all.reshape(query_all.shape[0], -1, HEAD)
    key_heads = key_all.reshape(length, -1, HEAD)
    value_heads = value_all.reshape(length, -1, HEAD)

    def scores_of():
        return (
            jnp.einsum("qhd,khd->hqk", query_heads, key_heads, preferred_element_type=jnp.float32)
            * factor
        )

    masked = jnp.where(allowed[None], scores_of(), NEGATIVE)
    top = jnp.max(masked, axis=-1)
    weights = jnp.where(allowed[None], jnp.exp(masked - top[..., None]), 0.0)
    total = jnp.sum(weights, axis=-1)
    added = jnp.einsum(
        "hqk,khd->qhd", weights.astype(jnp.bfloat16), value_heads, preferred_element_type=jnp.float32
    )
    context = added / total.T[:, :, None]
    log_total = top + jnp.log(total)
    context_all = context.reshape(context.shape[0], -1).astype(jnp.bfloat16)
    context_low = to_blocks([context_all], blocks)[0] if spread else context_all

    attended = hidden_float + pair_sum(dot_rows(context_low, full_output))
    mid_low = rms_scale(attended, mid_gain).astype(jnp.bfloat16)

    cot_float = cotangent.astype(jnp.float32)
    full_gate = ffn_full[:, :padded]
    full_up = ffn_full[:, padded : 2 * padded]
    full_down = ffn_full[:, 2 * padded :]
    gate = plain_dot(mid_low, full_gate)
    upward = plain_dot(mid_low, full_up)
    sigma = jax.nn.sigmoid(gate)
    silu_gate = gate * sigma
    act_low = (silu_gate * upward).astype(jnp.bfloat16)
    act_grad = plain_dot(cotangent, full_down)
    gate_grad_low = (act_grad * upward * sigma * (1.0 + gate * (1.0 - sigma))).astype(jnp.bfloat16)
    up_grad_low = (act_grad * silu_gate).astype(jnp.bfloat16)
    mid_part = dot_rows(gate_grad_low, full_gate) + dot_rows(up_grad_low, full_up)
    ffn_part = dot_rows(act_low, full_down)
    mid_grad = pair_sum(mid_part)
    output = (attended + pair_sum(ffn_part)).astype(jnp.bfloat16)
    attended_norm_grad, mid_gain_grad = jax.vjp(rms_scale, attended, mid_gain)[1](mid_grad)
    attended_grad = cot_float + attended_norm_grad

    resid_low = attended_grad.astype(jnp.bfloat16)
    context_grad_low = plain_dot(resid_low, full_output).astype(jnp.bfloat16)
    if spread:
        context_grad_all = to_heads([context_grad_low], blocks)[0]
    else:
        context_grad_all = context_grad_low
    context_grad_heads = context_grad_all.reshape(context_grad_all.shape[0], -1, HEAD)
    delta = jnp.sum(context_grad_heads.astype(jnp.float32) * context, axis=-1).T
    probs = jnp.where(allowed[None], jnp.exp(scores_of() - log_total[..., None]), 0.0)
    probs_low = probs.astype(jnp.bfloat16)
    prob_grad = jnp.einsum(
        "qhd,khd->hqk", context_grad_heads, value_heads, preferred_element_type=jnp.float32
    )
    score_grad = (probs * (prob_grad - delta[..., None])).astype(jnp.bfloat16)
    query_grad = (
        jnp.einsum("hqk,khd->qhd", score_grad, key_heads, preferred_element_type=jnp.float32)
        * factor
    )
    key_grad = (
        jnp.einsum("hqk,qhd->khd", score_grad, query_heads, preferred_element_type=jnp.float32)
        * factor
    )
    value_grad = jnp.einsum(
        "hqk,qhd->khd", probs_low, context_grad_heads, preferred_element_type=jnp.float32
    )
    query_grad, key_grad, value_grad = (
        grad.reshape(grad.shape[0], -1).astype(jnp.bfloat16)
        for grad in (query_grad, key_grad, value_grad)
    )
    if spread:
        query_grad_low, key_grad_low, value_grad_low = to_blocks(
            [query_grad, key_grad, value_grad], blocks
        )
    else:
        query_grad_low = query_grad
        mine = lax.psum_scatter(
            jnp.concatenate([key_grad, value_grad], axis=1), "blk", scatter_dimension=0, tiled=True
        )
        key_grad_low, value_grad_low = mine[:, :width], mine[:, width:]

    normed_grad = pair_sum(dot_rows(query_grad_low, full_query))
    memory_in_grad = pair_sum(
        dot_rows(key_grad_low, full_key) + dot_rows(value_grad_low, full_value)
    )
    shares = fold_products(
        [
            (mid_low, [gate_grad_low, up_grad_low]),
            (cotangent, [act_low]),
            (resid_low, [context_low]),
            (normed_low, [query_grad_low]),
            (memory_low, [key_grad_low, value_grad_low]),
        ],
        0,
    )
    gate_share, up_share = shares[0]
    (down_share,), (output_share,), (query_share,) = shares[1:4]
    key_share, value_share = shares[4]
    gate_share, up_share, down_share = (
        share[:, :hidden_units] for share in (gate_share, up_share, down_share)
    )
    hidden_norm_grad, input_gain_grad = jax.vjp(rms_scale, hidden_float, input_gain)[1](normed_grad)
    memory_grad, source_gain_grad = jax.vjp(rms_scale, memory_float, source_gain)[1](memory_in_grad)
    hidden_grad = attended_grad + hidden_norm_grad
    gain_shares = fold_vector(jnp.stack([input_gain_grad, source_gain_grad, mid_gain_grad], axis=0))
    return (
        output,
        hidden_grad,
        memory_grad,
        query_share,
        key_share,
        value_share,
        output_share,
        gate_share,
        up_share,
        down_share,
        gain_shares[0],
        gain_shares[1],
        gain_shares[2],
    )


def solution(mesh):
    tokens = P(("dp", "blk"), None)
    weight = P(("dp", "blk"), "heads")
    gain = P(("dp", "blk"))
    return jax.shard_map(
        local,
        mesh=mesh,
        in_specs=(tokens, tokens, P("dp", None)) + (weight,) * 7 + (gain,) * 3 + (tokens,),
        out_specs=(tokens,) * 3 + (weight,) * 7 + (gain,) * 3,
        check_vma=False,
    )
```

```python
import functools
import math

import jax
import jax.numpy as jnp
from jax import lax
from jax.experimental import pallas as pl
from jax.experimental.pallas import tpu as pltpu
from jax.sharding import PartitionSpec as P

MESH = pl.DeviceIdType.MESH
HEAD = 128
LANES = 128
MARKS = (7, 13)
STRIPS = 16
LAST_MARKS = (8, 15)
MESH_AXES = ("dp", "blk", "heads")
EPSILON = 1e-06
NEGATIVE = -1e30


def rms_scale(values, gain):
    return values * lax.rsqrt(jnp.mean(values * values, axis=-1, keepdims=True) + EPSILON) * gain


def plain_dot(left, right):
    return jnp.dot(left, right, preferred_element_type=jnp.float32)


def dot_rows(left, right):
    return lax.dot_general(
        left, right, (((1,), (1,)), ((), ())), preferred_element_type=jnp.float32
    )


def dot_cols(left, right):
    return lax.dot_general(
        left, right, (((0,), (0,)), ((), ())), preferred_element_type=jnp.float32
    )


def swap(array, axis, bit):
    size = lax.axis_size(axis)
    return lax.ppermute(array, axis, [(i, i ^ bit) for i in range(size)])


def heads_other(low):
    if lax.axis_size("heads") == 2:
        return swap(low, "heads", 1)
    return (lax.psum(low.astype(jnp.float32), "heads") - low.astype(jnp.float32)).astype(low.dtype)


def pair_add(low, other):
    return low.astype(jnp.float32) + other.astype(jnp.float32)


def pair_sum(part):
    low = part.astype(jnp.bfloat16)
    return pair_add(low, heads_other(low))


def fold_steps():
    steps = []
    for axis in ("dp", "blk"):
        size, bit = lax.axis_size(axis), 1
        while bit < size:
            steps.append((axis, bit))
            bit *= 2
    return steps


def late_steps(steps):
    first = [step for step in steps if step[0] == "dp"][1:]
    return [step for step in steps if step not in first] + first


def fold_order(width, steps):
    shards = 2 ** len(steps)
    part = width // shards
    offsets = []
    for place in range(shards):
        at = {axis: lax.axis_index(axis) for axis in ("dp", "blk")}
        for number, (axis, bit) in enumerate(steps):
            if place >> (len(steps) - 1 - number) & 1:
                at[axis] = flipped(at[axis], bit)
        offsets.append((at["dp"] * lax.axis_size("blk") + at["blk"]) * part)
    return offsets, part


def flipped(index, bit):
    return index + bit * (1 - 2 * ((index // bit) % 2))


def fold_engine(plans, edges, tiles, width, slots, period, lags, left_refs, right_ref, out_ref, scratch):
    count = len(plans[0])
    held, load_sem, send_sem, recv_sem, credit = scratch[:5]
    sent, got = scratch[5 : 5 + count], scratch[5 + count : 5 + 2 * count]
    lefts, features = held.shape[1:3]
    here = [lax.axis_index(axis) for axis in MESH_AXES]
    partners = [
        [
            tuple(
                flipped(place, bit) if name == axis else place
                for name, place in zip(MESH_AXES, here)
            )
            for axis, bit in steps
        ]
        for steps in plans
    ]
    loads = []
    for plan, steps in enumerate(plans):
        offsets, part = fold_order(features, steps)
        for number in range(lefts):
            for place, offset in enumerate(offsets):
                loads.append(
                    pltpu.make_async_copy(
                        left_refs[number].at[pl.ds(pl.multiple_of(offset, part), part)],
                        held.at[plan, number, pl.ds(place * part, part)],
                        load_sem.at[plan, number, place],
                    )
                )

    def plan_of(tile):
        return jnp.where(lax.rem(tile, period) == period - 1, 1, 0) if len(plans) > 1 else 0

    def partner_of(step, plan):
        if len(plans) == 1:
            return partners[0][step]
        return tuple(
            usual + plan * (other - usual)
            for usual, other in zip(partners[0][step], partners[1][step])
        )

    def transfer(step, tile):
        return pltpu.make_async_remote_copy(
            src_ref=sent[step].at[lax.rem(tile, 2)],
            dst_ref=got[step].at[lax.rem(tile, slots)],
            send_sem=send_sem.at[step, lax.rem(tile, 2)],
            recv_sem=recv_sem.at[step, lax.rem(tile, slots)],
            device_id=partner_of(step, plan_of(tile)),
            device_id_type=MESH,
        )

    def stage(number, tile):
        slot = lax.rem(tile, slots)
        plan = plan_of(tile)
        if number > 0:
            transfer(number - 1, tile).wait_recv()
        last = number == count
        low = 0 if last else features >> (number + 1)
        high = features >> number
        group = jnp.int32(0)
        for edge in edges:
            group = group + (tile >= edge).astype(jnp.int32)
        columns = pl.ds(pl.multiple_of(tile * width, width), width)
        total = jnp.dot(
            held[plan, group, low:high], right_ref[:, columns], preferred_element_type=jnp.float32
        )
        for earlier in range(number):
            total = total + got[earlier][slot, low:high].astype(jnp.float32)
        if last:
            out_ref[:, columns] = total

            @pl.when(tile < tiles - slots)
            def _():
                for step in range(count):
                    pl.semaphore_signal(
                        credit.at[plan, step],
                        inc=1,
                        device_id=partner_of(step, plan),
                        device_id_type=MESH,
                    )

            return

        @pl.when(tile >= 2)
        def _():
            transfer(number, tile - 2).wait_send()

        sent[number][lax.rem(tile, 2)] = total.astype(jnp.bfloat16)

        @pl.when(tile >= slots)
        def _():
            pl.semaphore_wait(credit.at[plan, number], 1)

        transfer(number, tile).start()

    def turn(index):
        for number in range(count + 1):
            tile = index - lags[number]

            @pl.when((tile >= 0) & (tile < tiles))
            def _(number=number, tile=tile):
                stage(number, tile)

    def finish():
        for step in range(count):
            for tile in range(max(0, tiles - 2), tiles):
                transfer(step, jnp.int32(tile)).wait_send()

    return loads, turn, finish, partners[0]


def greet(partners):
    barrier = pltpu.get_barrier_semaphore()
    for partner in partners:
        pl.semaphore_signal(barrier, inc=1, device_id=partner, device_id_type=MESH)
    pl.semaphore_wait(barrier, len(partners))


def fold_kernel(fold, lefts, *refs):
    left_refs, right_ref, out_ref, scratch = refs[:lefts], refs[lefts], refs[lefts + 1], refs[lefts + 2 :]
    loads, turn, finish, partners = fold_engine(*fold, left_refs, right_ref, out_ref, scratch)
    for load in loads:
        load.start()
    greet(partners)
    for load in loads:
        load.wait()

    def body(index, carry):
        turn(index)
        return carry

    lax.fori_loop(0, fold[2] + fold[6][-1], body, 0)
    finish()


def fold_lags(count):
    return (0,) + tuple(range(1, 2 * count, 2))


def fold_scratch(plans, lefts, features, rows, width, slots):
    count = len(plans[0])
    sizes = [features >> (step + 1) for step in range(count)]
    return [
        pltpu.VMEM((len(plans), lefts, features, rows), jnp.bfloat16),
        pltpu.SemaphoreType.DMA((len(plans), lefts, 1 << count)),
        pltpu.SemaphoreType.DMA((count, 2)),
        pltpu.SemaphoreType.DMA((count, slots)),
        pltpu.SemaphoreType.REGULAR((len(plans), count)),
        *[pltpu.VMEM((2, size, width), jnp.bfloat16) for size in sizes],
        *[pltpu.VMEM((slots, size, width), jnp.bfloat16) for size in sizes],
    ]


def fold_setting(groups, width, slots, period):
    steps = fold_steps()
    plans = [steps]
    if lax.axis_size("dp") > 2 and period and slots % period == 0:
        plans.append(late_steps(steps))
    edges, tiles = [], 0
    for _, many in groups:
        tiles += sum(right.shape[1] for right in many) // width
        edges.append(tiles)
    lefts = [left for left, _ in groups]
    rights = [right for _, many in groups for right in many]
    rights = rights[0] if len(rights) == 1 else jnp.concatenate(rights, axis=1)
    fold = (plans, edges[:-1], tiles, width, slots, period, fold_lags(len(steps)))
    features, rows = lefts[0].shape
    shape = jax.ShapeDtypeStruct((features >> len(steps), tiles * width), jnp.float32)
    scratch = fold_scratch(plans, len(lefts), features, rows, width, slots)
    cost = pl.CostEstimate(
        flops=2 * features * rows * tiles * width,
        bytes_accessed=tiles * width * features * 8,
        transcendentals=0,
    )
    return fold, lefts, rights, shape, scratch, cost


def remote_params(call):
    return pltpu.CompilerParams(
        collective_id=call, has_side_effects=True, vmem_limit_bytes=63 * 1024 * 1024
    )


def fold_products(groups, call, width=256, slots=12, period=6):
    fold, lefts, rights, shape, scratch, cost = fold_setting(groups, width, slots, period)
    folded = pl.pallas_call(
        functools.partial(fold_kernel, fold, len(lefts)),
        out_shape=shape,
        in_specs=[pl.BlockSpec(memory_space=pl.ANY)] * len(lefts)
        + [pl.BlockSpec(memory_space=pltpu.VMEM)],
        out_specs=pl.BlockSpec(memory_space=pltpu.VMEM),
        scratch_shapes=scratch,
        compiler_params=remote_params(call),
        cost_estimate=cost,
    )(*lefts, rights)
    return unstacked(groups, folded)


def unstacked(groups, folded):
    shares, at = [], 0
    for _, many in groups:
        shares.append([])
        for right in many:
            shares[-1].append(folded[:, at : at + right.shape[1]])
            at += right.shape[1]
    return shares


def together(*arrays):
    return lax.optimization_barrier(arrays)


def fold_vector(vector):
    steps = fold_steps()
    offsets, part = fold_order(vector.shape[-1], steps)
    held = jnp.stack(
        [lax.dynamic_slice_in_dim(vector, offset, part, axis=-1) for offset in offsets], axis=0
    )
    for axis, bit in steps:
        half = held.shape[0] // 2
        held = held[:half] + swap(held[half:], axis, bit)
    return held[0]


def to_heads(pieces, blocks):
    rows, width = pieces[0].shape
    part = width // blocks
    packed = jnp.stack(
        [
            jnp.concatenate([piece[:, i * part : (i + 1) * part] for piece in pieces], axis=1)
            for i in range(blocks)
        ],
        axis=0,
    )
    moved = lax.all_to_all(packed, "blk", 0, 0)
    return moved.reshape(rows * blocks, part * len(pieces))


def swap_blocks(packed, blocks):
    length, columns = packed.shape
    return lax.all_to_all(packed.reshape(blocks, length // blocks, columns), "blk", 0, 0)


def side_by_side(moved, count):
    part = moved.shape[2] // count
    return [
        jnp.concatenate(
            [moved[j, :, i * part : (i + 1) * part] for j in range(moved.shape[0])], axis=1
        )
        for i in range(count)
    ]


def first_allowed(doc_ends, positions):
    first = jnp.zeros(positions.shape, jnp.int32)
    for number in range(doc_ends.shape[0]):
        end = doc_ends[number]
        first = jnp.maximum(first, jnp.where(end <= positions, end, 0))
    return first


def tile_probs(ends, packed, part, head, start, stop, factor):
    own = slice(head * HEAD, (head + 1) * HEAD)
    keys = packed[:stop, part + own.start : part + own.stop]
    scores = dot_rows(packed[start:stop, own], keys) * factor
    positions = start + lax.broadcasted_iota(jnp.int32, (stop - start, 1), 0)
    first = first_allowed(ends, positions)
    key_pos = lax.broadcasted_iota(jnp.int32, scores.shape, 1)
    allowed = (key_pos >= first) & (key_pos <= positions)
    scores = jnp.where(allowed, scores, NEGATIVE)
    weights = jnp.exp(scores - jnp.max(scores, axis=-1, keepdims=True))
    return weights / jnp.sum(weights, axis=-1, keepdims=True)


def attend_kernel(part, tile, factor, ends, packed, out):
    for head in range(part // HEAD):
        own = slice(head * HEAD, (head + 1) * HEAD)
        for start in range(0, packed.shape[0], tile):
            stop = start + tile
            probs = tile_probs(ends, packed, part, head, start, stop, factor)
            values = packed[:stop, 2 * part + own.start : 2 * part + own.stop]
            out[start:stop, own] = plain_dot(probs.astype(jnp.bfloat16), values).astype(out.dtype)


def attend_back_head(part, tile, factor, head, ends, packed, grads, out, key_sum, value_sum):
    length = packed.shape[0]
    own = slice(head * HEAD, (head + 1) * HEAD)
    key_own = slice(part + own.start, part + own.stop)
    value_own = slice(2 * part + own.start, 2 * part + own.stop)
    for start in reversed(range(0, length, tile)):
        stop = start + tile
        probs = tile_probs(ends, packed, part, head, start, stop, factor)
        grad = grads[start:stop, own]
        prob_grad = dot_rows(grad, packed[:stop, value_own])
        delta = jnp.sum(probs * prob_grad, axis=-1, keepdims=True)
        score_grad = (probs * (prob_grad - delta)).astype(jnp.bfloat16)
        query_grad = plain_dot(score_grad, packed[:stop, key_own]) * factor
        out[start:stop, own] = query_grad.astype(out.dtype)
        key_part = dot_cols(score_grad, packed[start:stop, own])
        value_part = dot_cols(probs.astype(jnp.bfloat16), grad)
        if stop == length:
            key_sum[:stop] = key_part
            value_sum[:stop] = value_part
        else:
            key_sum[:stop] += key_part
            value_sum[:stop] += value_part
    out[:, key_own] = (key_sum[...] * factor).astype(out.dtype)
    out[:, value_own] = value_sum[...].astype(out.dtype)


def attention_tile(length):
    return next(tile for tile in (512, 384, 256, 128, 64, 32, 16) if length % tile == 0)


def attention_call(kernel, doc_ends, arrays, columns, scratch, matmuls):
    length, width = arrays[0].shape
    part = width // 3
    tile = attention_tile(length)
    vmem = pl.BlockSpec(memory_space=pltpu.VMEM)
    return pl.pallas_call(
        functools.partial(kernel, part, tile, 1.0 / math.sqrt(HEAD)),
        out_shape=jax.ShapeDtypeStruct((length, columns), jnp.bfloat16),
        in_specs=[pl.BlockSpec(memory_space=pltpu.SMEM)] + [vmem] * len(arrays),
        out_specs=vmem,
        scratch_shapes=scratch,
        compiler_params=pltpu.CompilerParams(vmem_limit_bytes=48 * 1024 * 1024),
        cost_estimate=pl.CostEstimate(
            flops=2 * matmuls * length * length * part,
            bytes_accessed=10 * length * width,
            transcendentals=length * length * part // HEAD,
        ),
    )(doc_ends, *arrays)


def attend(doc_ends, packed):
    return attention_call(attend_kernel, doc_ends, [packed], packed.shape[1] // 3, [], 2)


def middle_kernel(
    fold, marks, tile, factor, ends, first_left, second_left, right_ref, mid_ref, attended_ref, cot_ref,
    gain_ref, weight_ref, packed_ref, down_ref, out_ref, resid_ref, gain_out, moved, result, *scratch
):
    count = len(fold[0][0])
    attended, cot, weight, packed, load_sem = scratch[:5]
    other, sent_grads, grads, out, key_sum, value_sum = scratch[5:11]
    heads_sem, ctx_sem, out_sem, down, down_sem, ready = scratch[11:17]
    left_refs = (first_left, second_left)
    loads, turn, finish, partners = fold_engine(*fold, left_refs, right_ref, out_ref, scratch[17:])
    rows, features = mid_ref.shape
    blocks, _, part = sent_grads.shape
    dp, blk, heads = (lax.axis_index(axis) for axis in MESH_AXES)

    def away(distance):
        at, bit = blk, 1
        while bit <= distance:
            if distance & bit:
                at = flipped(at, bit)
            bit *= 2
        return at

    mirror = (dp, blk, flipped(heads, 1))
    met = partners + [mirror]
    met += [(dp, away(d), heads) for d in range(1, blocks) if d & (d - 1)]
    loads = loads + [
        pltpu.make_async_copy(source, target, load_sem.at[number])
        for number, (source, target) in enumerate(
            [(attended_ref, attended), (cot_ref, cot), (weight_ref, weight), (packed_ref, packed)]
        )
    ]
    for load in loads:
        load.start()
    greet(met)
    mirrored = pltpu.make_async_remote_copy(
        src_ref=mid_ref,
        dst_ref=other,
        send_sem=heads_sem.at[0],
        recv_sem=heads_sem.at[1],
        device_id=mirror,
        device_id_type=MESH,
    )
    mirrored.start()
    for load in loads:
        load.wait()

    def block(index):
        return pl.ds(pl.multiple_of(index * rows, rows), rows)

    def ctx_copy(distance, landing):
        return pltpu.make_async_remote_copy(
            src_ref=sent_grads.at[away(distance)],
            dst_ref=grads.at[block(landing)],
            send_sem=ctx_sem.at[0, distance],
            recv_sem=ctx_sem.at[1, distance],
            device_id=(dp, away(distance), heads),
            device_id_type=MESH,
        )

    def landing_of(kind, source):
        offset = kind * (part * blocks) + source * part
        return moved.at[:, pl.ds(pl.multiple_of(offset, part), part)]

    def out_copy(kind, distance, landing):
        return pltpu.make_async_remote_copy(
            src_ref=out.at[block(away(distance)), pl.ds(kind * part, part)],
            dst_ref=landing_of(kind, landing),
            send_sem=out_sem.at[0, kind, distance],
            recv_sem=out_sem.at[1, kind, distance],
            device_id=(dp, away(distance), heads),
            device_id_type=MESH,
        )

    step = rows // 3 if rows % 48 == 0 else rows
    starts = list(range(0, rows, step))

    def norm_back(start):
        if start == 0:
            mirrored.wait()
        for start in (start,):
            own = slice(start, start + step)
            values = attended[own]
            mid_grad = pair_add(mid_ref[own], other[own])
            scale = lax.rsqrt(jnp.mean(values * values, axis=-1, keepdims=True) + EPSILON)
            normed = values * scale
            scaled = mid_grad * gain_ref[...]
            inner = jnp.mean(scaled * normed, axis=-1, keepdims=True)
            total = cot[own].astype(jnp.float32) + scale * (scaled - normed * inner)
            resid_ref[own] = total
            gain_part = jnp.sum(mid_grad * normed, axis=0, keepdims=True)
            if start == 0:
                gain_out[...] = gain_part
            else:
                gain_out[...] += gain_part
            low = plain_dot(total.astype(jnp.bfloat16), weight[...]).astype(jnp.bfloat16)
            for number in range(blocks):
                sent_grads[number, own] = low[:, number * part : (number + 1) * part]
        if start != starts[-1]:
            return
        grads[block(blk)] = sent_grads[blk]
        for distance in range(1, blocks):
            ctx_copy(distance, blk).start()

    strip = down.shape[1]
    strips = features // strip
    units = down.shape[2]
    down_at, act_at = down_ref.shape[1] - units, right_ref.shape[1] - units
    second = pltpu.make_async_remote_copy(
        src_ref=cot,
        dst_ref=other,
        send_sem=heads_sem.at[2],
        recv_sem=heads_sem.at[3],
        device_id=mirror,
        device_id_type=MESH,
    )

    def strip_copy(number):
        slot = lax.rem(number, 2)
        return pltpu.make_async_copy(
            down_ref.at[pl.ds(pl.multiple_of(number * strip, strip), strip), pl.ds(down_at, units)],
            down.at[slot],
            down_sem.at[slot],
        )

    def strip_step(number):
        strip_copy(number).wait()

        @pl.when(number + 1 < strips)
        def _():
            strip_copy(number + 1).start()

        columns = pl.ds(pl.multiple_of(number * strip, strip), strip)
        product = dot_rows(right_ref[:, act_at:], down[lax.rem(number, 2)])
        cot[:, columns] = product.astype(jnp.bfloat16)

    def one_head(head):
        attend_back_head(part, tile, factor, head, ends, packed, grads, out, key_sum, value_sum)

    def body(index, carry):
        turn(index)

        for number, start in enumerate(starts):

            @pl.when(index == marks[0] + number)
            def _(start=start):
                norm_back(start)

        done = marks[0] + len(starts) - 1

        @pl.when(index == done)
        def _():
            pl.semaphore_signal(ready, inc=1, device_id=mirror, device_id_type=MESH)
            strip_copy(jnp.int32(0)).start()

        @pl.when((index > done) & (index <= done + strips))
        def _():
            strip_step(index - done - 1)

        @pl.when(index == done + strips)
        def _():
            pl.semaphore_wait(ready, 1)
            second.start()

        @pl.when(index == marks[1])
        def _():
            for distance in range(1, blocks):
                ctx_copy(distance, away(distance)).wait_recv()
                ctx_copy(distance, blk).wait_send()

        for head in range(part // HEAD):

            @pl.when(index == marks[1] + head)
            def _(head=head):
                one_head(head)

        @pl.when(index == marks[1] + part // HEAD - 1)
        def _():
            for kind in range(3):
                offset = pl.multiple_of(kind * (part * blocks) + blk * part, part)
                moved[:, pl.ds(offset, part)] = out[block(blk), kind * part : (kind + 1) * part]

        for number in range(3 * (blocks - 1)):

            @pl.when(index == marks[1] + part // HEAD + 2 * number)
            def _(kind=number // (blocks - 1), distance=number % (blocks - 1) + 1):
                out_copy(kind, distance, blk).start()

        return carry

    lax.fori_loop(0, fold[2] + fold[6][-1], body, 0)
    finish()
    second.wait()
    for start in starts:
        own = slice(start, start + step)
        result[own] = (attended[own] + pair_add(cot[own], other[own])).astype(result.dtype)
    for kind in range(3):
        for distance in range(1, blocks):
            out_copy(kind, distance, away(distance)).wait_recv()
            out_copy(kind, distance, blk).wait_send()


def middle(
    groups, doc_ends, mid, attended, cot, gain, weight, packed, down, call, marks, width=256, slots=10
):
    fold, lefts, rights, shape, scratch, cost = fold_setting(groups, width, slots, 0)
    blocks = lax.axis_size("blk")
    rows, features = mid.shape
    length, columns = packed.shape
    part = columns // 3
    tile = 256 if length % 256 == 0 else attention_tile(length)
    turns = fold[2] + fold[6][-1]
    assert marks[0] + 3 + STRIPS < turns and marks[0] + 3 < marks[1]
    assert marks[1] + part // HEAD + 2 * 3 * (blocks - 1) < turns
    vmem, anywhere = (pl.BlockSpec(memory_space=space) for space in (pltpu.VMEM, pl.ANY))
    low = jnp.bfloat16
    folded, resid, gain_grad, moved, result = pl.pallas_call(
        functools.partial(middle_kernel, fold, marks, tile, 1.0 / math.sqrt(HEAD)),
        out_shape=(
            shape,
            jax.ShapeDtypeStruct(attended.shape, jnp.float32),
            jax.ShapeDtypeStruct((1, features), jnp.float32),
            jax.ShapeDtypeStruct((rows, columns * blocks), low),
            jax.ShapeDtypeStruct((rows, features), low),
        ),
        in_specs=[
            pl.BlockSpec(memory_space=pltpu.SMEM),
            anywhere,
            anywhere,
            vmem,
            vmem,
            anywhere,
            anywhere,
            vmem,
            anywhere,
            anywhere,
            anywhere,
        ],
        out_specs=(vmem,) * 5,
        scratch_shapes=[
            pltpu.VMEM(attended.shape, jnp.float32),
            pltpu.VMEM(cot.shape, low),
            pltpu.VMEM(weight.shape, low),
            pltpu.VMEM(packed.shape, low),
            pltpu.SemaphoreType.DMA((4,)),
            pltpu.VMEM(mid.shape, low),
            pltpu.VMEM((blocks, rows, part), low),
            pltpu.VMEM((length, part), low),
            pltpu.VMEM((length, columns), low),
            pltpu.VMEM((length, HEAD), jnp.float32),
            pltpu.VMEM((length, HEAD), jnp.float32),
            pltpu.SemaphoreType.DMA((4,)),
            pltpu.SemaphoreType.DMA((2, blocks)),
            pltpu.SemaphoreType.DMA((2, 3, blocks)),
            pltpu.VMEM((2, features // STRIPS, groups[-1][1][0].shape[1]), low),
            pltpu.SemaphoreType.DMA((2,)),
            pltpu.SemaphoreType.REGULAR,
            *scratch,
        ],
        compiler_params=remote_params(call),
        cost_estimate=cost,
    )(doc_ends, *lefts, rights, mid, attended, cot, gain[None], weight, packed, down)
    return unstacked(groups, folded), resid, gain_grad[0], moved, result


def last_kernel(
    fold, marks, first_left, second_left, third_left, right_ref, normed_part, memory_part, hidden_ref,
    memory_ref, resid_ref, gains_ref, mid_gain_ref, out_ref, hidden_grad, memory_grad, gain_out, *scratch
):
    steps = fold[0][0]
    count = len(steps)
    normed_other, memory_other, hidden, memory, resid = scratch[:5]
    load_sem, heads_sem, gain_sem, gain_held = scratch[5:9]
    gain_got = scratch[9 : 9 + count]
    left_refs = (first_left, second_left, third_left)
    loads, turn, finish, partners = fold_engine(
        *fold, left_refs, right_ref, out_ref, scratch[9 + count :]
    )
    rows, features = normed_part.shape
    dp, blk, heads = (lax.axis_index(axis) for axis in MESH_AXES)
    mirror = (dp, blk, flipped(heads, 1))
    loads = loads + [
        pltpu.make_async_copy(source, target, load_sem.at[number])
        for number, (source, target) in enumerate(
            [(hidden_ref, hidden), (memory_ref, memory), (resid_ref, resid)]
        )
    ]
    for load in loads:
        load.start()
    greet(partners + [mirror])
    mirrored = [
        pltpu.make_async_remote_copy(
            src_ref=source,
            dst_ref=target,
            send_sem=heads_sem.at[0, number],
            recv_sem=heads_sem.at[1, number],
            device_id=mirror,
            device_id_type=MESH,
        )
        for number, (source, target) in enumerate(
            [(normed_part, normed_other), (memory_part, memory_other)]
        )
    ]
    for copy in mirrored:
        copy.start()
    for load in loads:
        load.wait()
    offsets, part = fold_order(features, steps)

    def keep_gain(number, gain_grad):
        for place, offset in enumerate(offsets):
            columns = pl.ds(pl.multiple_of(offset, part), part)
            gain_held[place, number : number + 1] = gain_grad[:, columns]

    def norm_back(number):
        mirrored[number].wait()
        own, other = ((normed_part, normed_other), (memory_part, memory_other))[number]
        source, target = ((hidden, hidden_grad), (memory, memory_grad))[number]
        step = rows // 3 if rows % 48 == 0 else rows
        gain_total = None
        for start in range(0, rows, step):
            here = slice(start, start + step)
            values = source[here].astype(jnp.float32)
            grad = pair_add(own[here], other[here])
            scale = lax.rsqrt(jnp.mean(values * values, axis=-1, keepdims=True) + EPSILON)
            normed = values * scale
            scaled = grad * gains_ref[number : number + 1]
            inner = jnp.mean(scaled * normed, axis=-1, keepdims=True)
            total = scale * (scaled - normed * inner)
            target[here] = total + resid[here] if number == 0 else total
            gain_part = jnp.sum(grad * normed, axis=0, keepdims=True)
            gain_total = gain_part if gain_total is None else gain_total + gain_part
        gain_sum[...] = gain_total
        keep_gain(number, gain_sum)

    gain_sum = scratch[-1]

    def gain_copy(step):
        half = (1 << count) >> (step + 1)
        return pltpu.make_async_remote_copy(
            src_ref=gain_held.at[pl.ds(half, half)],
            dst_ref=gain_got[step],
            send_sem=gain_sem.at[0, step],
            recv_sem=gain_sem.at[1, step],
            device_id=partners[step],
            device_id_type=MESH,
        )

    def gain_step(step):
        if step > 0:
            gain_copy(step - 1).wait()
            half = (1 << count) >> step
            gain_held[:half] += gain_got[step - 1][...]
        if step < count:
            gain_copy(step).start()

    def body(index, carry):
        turn(index)

        @pl.when(index == marks[0])
        def _():
            gain_held[...] = jnp.zeros_like(gain_held)
            keep_gain(2, mid_gain_ref)
            norm_back(0)

        @pl.when(index == marks[1])
        def _():
            norm_back(1)

        for step in range(count):

            @pl.when(index == marks[1] + step)
            def _(step=step):
                gain_step(step)

        return carry

    lax.fori_loop(0, fold[2] + fold[6][-1], body, 0)
    gain_step(count)
    gain_out[...] = gain_held[0]
    finish()


def last(groups, normed_part, memory_part, hidden, memory, resid, gains, mid_gain_grad, call, marks, width=256, slots=12):
    fold, lefts, rights, shape, scratch, cost = fold_setting(groups, width, slots, 6)
    count = len(fold[0][0])
    marks = tuple(min(mark, fold[2] + fold[6][-1] - count) for mark in marks)
    rows, features = normed_part.shape
    part = features >> count
    vmem, anywhere = (pl.BlockSpec(memory_space=space) for space in (pltpu.VMEM, pl.ANY))
    folded, hidden_grad, memory_grad, gain_grads = pl.pallas_call(
        functools.partial(last_kernel, fold, marks),
        out_shape=(
            shape,
            jax.ShapeDtypeStruct(hidden.shape, jnp.float32),
            jax.ShapeDtypeStruct(hidden.shape, jnp.float32),
            jax.ShapeDtypeStruct((8, part), jnp.float32),
        ),
        in_specs=[anywhere] * 3 + [vmem] * 3 + [anywhere] * 3 + [vmem] * 2,
        out_specs=(vmem,) * 4,
        scratch_shapes=[
            pltpu.VMEM(hidden.shape, jnp.bfloat16),
            pltpu.VMEM(hidden.shape, jnp.bfloat16),
            pltpu.VMEM(hidden.shape, jnp.bfloat16),
            pltpu.VMEM(hidden.shape, jnp.bfloat16),
            pltpu.VMEM(hidden.shape, jnp.float32),
            pltpu.SemaphoreType.DMA((3,)),
            pltpu.SemaphoreType.DMA((2, 2)),
            pltpu.SemaphoreType.DMA((2, count)),
            pltpu.VMEM((1 << count, 8, part), jnp.float32),
            *[pltpu.VMEM(((1 << count) >> (step + 1), 8, part), jnp.float32) for step in range(count)],
            *scratch,
            pltpu.VMEM((1, features), jnp.float32),
        ],
        compiler_params=remote_params(call),
        cost_estimate=cost,
    )(*lefts, rights, normed_part, memory_part, hidden, memory, resid, gains, mid_gain_grad[None])
    return unstacked(groups, folded), hidden_grad, memory_grad, gain_grads


def by_head(array):
    return array.reshape(array.shape[0], -1, HEAD).transpose(1, 0, 2)


def from_heads(array):
    return array.transpose(1, 0, 2).reshape(array.shape[1], -1).astype(jnp.bfloat16)


def plain_probs(doc_ends, query_pos, query, key):
    key_pos = jnp.arange(key.shape[0], dtype=jnp.int32)
    first = first_allowed(doc_ends, query_pos)
    allowed = (key_pos[None, :] >= first[:, None]) & (key_pos[None, :] <= query_pos[:, None])
    scores = dot_rows(query, key) * (1.0 / math.sqrt(HEAD))
    return jax.nn.softmax(jnp.where(allowed, scores, NEGATIVE), axis=-1)


def plain_attend(doc_ends, query_pos, queries, keys, values):
    def one(arrays):
        query, key, value = arrays
        probs = plain_probs(doc_ends, query_pos, query, key)
        return plain_dot(probs.astype(jnp.bfloat16), value)

    return from_heads(lax.map(one, (by_head(queries), by_head(keys), by_head(values))))


def plain_attend_back(doc_ends, query_pos, queries, keys, values, grads):
    factor = 1.0 / math.sqrt(HEAD)

    def one(arrays):
        query, key, value, grad = arrays
        probs = plain_probs(doc_ends, query_pos, query, key)
        prob_grad = dot_rows(grad, value)
        delta = jnp.sum(probs * prob_grad, axis=-1, keepdims=True)
        score_grad = (probs * (prob_grad - delta)).astype(jnp.bfloat16)
        return (
            plain_dot(score_grad, key) * factor,
            dot_cols(score_grad, query) * factor,
            dot_cols(probs.astype(jnp.bfloat16), grad),
        )

    arrays = tuple(by_head(array) for array in (queries, keys, values, grads))
    return tuple(from_heads(grad) for grad in lax.map(one, arrays))


def local(
    hidden_in,
    memory,
    lengths,
    query_weight,
    key_weight,
    value_weight,
    output_weight,
    gate_weight,
    up_weight,
    down_weight,
    attention_gain,
    memory_gain,
    feedforward_gain,
    cotangent,
):
    rows, features = hidden_in.shape
    blocks = lax.axis_size("blk")
    width = query_weight.shape[1]
    hidden_units = gate_weight.shape[1]
    heads_local = width // HEAD
    spread = heads_local % blocks == 0 and lax.axis_size("heads") == 2
    doc_ends = jnp.cumsum(lengths[0], dtype=jnp.int32)

    gains = jnp.stack([attention_gain, memory_gain, feedforward_gain], axis=1)
    gains = jnp.pad(gains, ((0, 0), (0, LANES - gains.shape[1])))
    attn_mine = jnp.concatenate(
        [query_weight, key_weight, value_weight, output_weight, gains], axis=1
    )
    attn_full = lax.all_gather(attn_mine, ("dp", "blk"), axis=0, tiled=True)
    padded = -(-hidden_units // (2 * LANES)) * (2 * LANES)
    ffn_mine = jnp.concatenate(
        [
            jnp.pad(weight, ((0, 0), (0, padded - hidden_units)))
            for weight in (gate_weight, up_weight, down_weight)
        ],
        axis=1,
    )
    ffn_mine, attn_full = together(ffn_mine, attn_full)
    ffn_full = lax.all_gather(ffn_mine, ("dp", "blk"), axis=0, tiled=True)

    full_query = attn_full[:, :width]
    full_key = attn_full[:, width : 2 * width]
    full_value = attn_full[:, 2 * width : 3 * width]
    full_output = attn_full[:, 3 * width : 4 * width]
    full_gains = attn_full[:, 4 * width : 4 * width + 3].astype(jnp.float32).T
    input_gain, source_gain, mid_gain = full_gains[0], full_gains[1], full_gains[2]

    hidden_float = hidden_in.astype(jnp.float32)
    memory_float = memory.astype(jnp.float32)
    memory_low = rms_scale(memory_float, source_gain).astype(jnp.bfloat16)
    normed_low = rms_scale(hidden_float, input_gain).astype(jnp.bfloat16)
    key_low = plain_dot(memory_low, full_key).astype(jnp.bfloat16)
    value_low = plain_dot(memory_low, full_value).astype(jnp.bfloat16)
    query_low = plain_dot(normed_low, full_query).astype(jnp.bfloat16)

    if spread:
        packed = to_heads([query_low, key_low, value_low], blocks)
        context_low = side_by_side(swap_blocks(attend(doc_ends, packed), blocks), 1)[0]
    else:
        query_pos = lax.axis_index("blk") * rows + jnp.arange(rows, dtype=jnp.int32)
        key_all = lax.all_gather(key_low, "blk", axis=0, tiled=True)
        value_all = lax.all_gather(value_low, "blk", axis=0, tiled=True)
        context_low = plain_attend(doc_ends, query_pos, query_low, key_all, value_all)

    attended = hidden_float + pair_sum(dot_rows(context_low, full_output))
    attended, cot_turned, normed_turned, memory_turned = together(
        attended, cotangent.T, normed_low.T, memory_low.T
    )
    mid_low = rms_scale(attended, mid_gain).astype(jnp.bfloat16)

    full_gate = ffn_full[:, :padded]
    full_up = ffn_full[:, padded : 2 * padded]
    full_down = ffn_full[:, 2 * padded :]
    gate = plain_dot(mid_low, full_gate)
    upward = plain_dot(mid_low, full_up)
    sigma = jax.nn.sigmoid(gate)
    silu_gate = gate * sigma
    act_low = (silu_gate * upward).astype(jnp.bfloat16)
    act_grad = plain_dot(cotangent, full_down)
    gate_grad_low = (act_grad * upward * sigma * (1.0 + gate * (1.0 - sigma))).astype(jnp.bfloat16)
    up_grad_low = (act_grad * silu_gate).astype(jnp.bfloat16)
    mid_part = dot_rows(gate_grad_low, full_gate) + dot_rows(up_grad_low, full_up)
    mid_part = mid_part.astype(jnp.bfloat16)
    products = [(mid_low.T, [gate_grad_low, up_grad_low]), (cot_turned, [act_low])]
    if spread:
        shares, attended_grad, mid_gain_grad, moved, output = middle(
            products,
            doc_ends,
            mid_part,
            attended,
            cotangent,
            mid_gain,
            full_output,
            packed,
            ffn_full,
            0,
            MARKS,
        )
        resid_low = attended_grad.astype(jnp.bfloat16)
        query_grad_low, key_grad_low, value_grad_low = (
            moved[:, i * width : (i + 1) * width] for i in range(3)
        )
    else:
        shares = fold_products(products, 0)
        output = (attended + pair_sum(dot_rows(act_low, full_down))).astype(jnp.bfloat16)
        mid_grad = pair_sum(mid_part)
        attended_norm_grad, mid_gain_grad = jax.vjp(rms_scale, attended, mid_gain)[1](mid_grad)
        attended_grad = cotangent.astype(jnp.float32) + attended_norm_grad
        resid_low = attended_grad.astype(jnp.bfloat16)
        context_grad_low = plain_dot(resid_low, full_output).astype(jnp.bfloat16)
        query_grad_low, key_grad, value_grad = plain_attend_back(
            doc_ends, query_pos, query_low, key_all, value_all, context_grad_low
        )
        moved = lax.psum_scatter(
            jnp.concatenate([key_grad, value_grad], axis=1), "blk", scatter_dimension=0, tiled=True
        )
        key_grad_low, value_grad_low = moved[:, :width], moved[:, width:]
    (gate_share, up_share), (down_share,) = shares
    normed_part = dot_rows(query_grad_low, full_query).astype(jnp.bfloat16)
    memory_part = (
        dot_rows(key_grad_low, full_key) + dot_rows(value_grad_low, full_value)
    ).astype(jnp.bfloat16)
    if spread:
        right_sets = ([context_low], [moved[:, :width]], [moved[:, width:]])
    else:
        right_sets = ([context_low], [query_grad_low], [key_grad_low, value_grad_low])
    products = list(zip((resid_low.T, normed_turned, memory_turned), right_sets))
    if spread:
        shares, hidden_grad, memory_grad, gain_shares = last(
            products,
            normed_part,
            memory_part,
            hidden_in,
            memory,
            attended_grad,
            jnp.stack([input_gain, source_gain], axis=0),
            mid_gain_grad,
            1,
            LAST_MARKS,
        )
    else:
        shares = fold_products(products, 1)
        normed_grad = pair_sum(normed_part)
        memory_in_grad = pair_sum(memory_part)
        hidden_norm_grad, input_gain_grad = jax.vjp(rms_scale, hidden_float, input_gain)[1](
            normed_grad
        )
        memory_grad, source_gain_grad = jax.vjp(rms_scale, memory_float, source_gain)[1](
            memory_in_grad
        )
        hidden_grad = attended_grad + hidden_norm_grad
        gain_shares = fold_vector(
            jnp.stack([input_gain_grad, source_gain_grad, mid_gain_grad], axis=0)
        )
    (output_share,), (query_share,), both = shares
    both = jnp.concatenate(both, axis=1)
    key_share, value_share = both[:, :width], both[:, width:]
    gate_share, up_share, down_share = (
        share[:, :hidden_units] for share in (gate_share, up_share, down_share)
    )
    return (
        output,
        hidden_grad,
        memory_grad,
        query_share,
        key_share,
        value_share,
        output_share,
        gate_share,
        up_share,
        down_share,
        gain_shares[0],
        gain_shares[1],
        gain_shares[2],
    )


def solution(mesh):
    tokens = P(("dp", "blk"), None)
    weight = P(("dp", "blk"), "heads")
    gain = P(("dp", "blk"))
    return jax.shard_map(
        local,
        mesh=mesh,
        in_specs=(tokens, tokens, P("dp", None)) + (weight,) * 7 + (gain,) * 3 + (tokens,),
        out_specs=(tokens,) * 3 + (weight,) * 7 + (gain,) * 3,
        check_vma=False,
    )
```

```python
import functools
import math

import jax
import jax.numpy as jnp
from jax import lax
from jax.experimental import pallas as pl
from jax.experimental.pallas import tpu as pltpu
from jax.sharding import PartitionSpec as P

MESH = pl.DeviceIdType.MESH
HEAD = 128
LANES = 128
MARKS = (7, 13)
STRIPS = 16
LAST_MARKS = (8, 15)
MESH_AXES = ("dp", "blk", "heads")
EPSILON = 1e-06
NEGATIVE = -1e30


def rms_scale(values, gain):
    return values * lax.rsqrt(jnp.mean(values * values, axis=-1, keepdims=True) + EPSILON) * gain


def plain_dot(left, right):
    return jnp.dot(left, right, preferred_element_type=jnp.float32)


def dot_rows(left, right):
    return lax.dot_general(
        left, right, (((1,), (1,)), ((), ())), preferred_element_type=jnp.float32
    )


def dot_cols(left, right):
    return lax.dot_general(
        left, right, (((0,), (0,)), ((), ())), preferred_element_type=jnp.float32
    )


def swap(array, axis, bit):
    size = lax.axis_size(axis)
    return lax.ppermute(array, axis, [(i, i ^ bit) for i in range(size)])


def heads_other(low):
    if lax.axis_size("heads") == 2:
        return swap(low, "heads", 1)
    return (lax.psum(low.astype(jnp.float32), "heads") - low.astype(jnp.float32)).astype(low.dtype)


def pair_add(low, other):
    return low.astype(jnp.float32) + other.astype(jnp.float32)


def pair_sum(part):
    low = part.astype(jnp.bfloat16)
    return pair_add(low, heads_other(low))


def fold_steps():
    steps = []
    for axis in ("dp", "blk"):
        size, bit = lax.axis_size(axis), 1
        while bit < size:
            steps.append((axis, bit))
            bit *= 2
    return steps


def late_steps(steps):
    first = [step for step in steps if step[0] == "dp"][1:]
    return [step for step in steps if step not in first] + first


def fold_order(width, steps):
    shards = 2 ** len(steps)
    part = width // shards
    offsets = []
    for place in range(shards):
        at = {axis: lax.axis_index(axis) for axis in ("dp", "blk")}
        for number, (axis, bit) in enumerate(steps):
            if place >> (len(steps) - 1 - number) & 1:
                at[axis] = flipped(at[axis], bit)
        offsets.append((at["dp"] * lax.axis_size("blk") + at["blk"]) * part)
    return offsets, part


def flipped(index, bit):
    return index + bit * (1 - 2 * ((index // bit) % 2))


def fold_engine(plans, edges, tiles, width, slots, period, lags, left_refs, right_ref, out_ref, scratch):
    count = len(plans[0])
    held, load_sem, send_sem, recv_sem, credit = scratch[:5]
    sent, got = scratch[5 : 5 + count], scratch[5 + count : 5 + 2 * count]
    lefts, features = held.shape[1:3]
    here = [lax.axis_index(axis) for axis in MESH_AXES]
    partners = [
        [
            tuple(
                flipped(place, bit) if name == axis else place
                for name, place in zip(MESH_AXES, here)
            )
            for axis, bit in steps
        ]
        for steps in plans
    ]
    loads = []
    for plan, steps in enumerate(plans):
        offsets, part = fold_order(features, steps)
        for number in range(lefts):
            for place, offset in enumerate(offsets):
                loads.append(
                    pltpu.make_async_copy(
                        left_refs[number].at[pl.ds(pl.multiple_of(offset, part), part)],
                        held.at[plan, number, pl.ds(place * part, part)],
                        load_sem.at[plan, number, place],
                    )
                )

    def plan_of(tile):
        return jnp.where(lax.rem(tile, period) == period - 1, 1, 0) if len(plans) > 1 else 0

    def partner_of(step, plan):
        if len(plans) == 1:
            return partners[0][step]
        return tuple(
            usual + plan * (other - usual)
            for usual, other in zip(partners[0][step], partners[1][step])
        )

    def transfer(step, tile):
        return pltpu.make_async_remote_copy(
            src_ref=sent[step].at[lax.rem(tile, 2)],
            dst_ref=got[step].at[lax.rem(tile, slots)],
            send_sem=send_sem.at[step, lax.rem(tile, 2)],
            recv_sem=recv_sem.at[step, lax.rem(tile, slots)],
            device_id=partner_of(step, plan_of(tile)),
            device_id_type=MESH,
        )

    def stage(number, tile):
        slot = lax.rem(tile, slots)
        plan = plan_of(tile)
        if number > 0:
            transfer(number - 1, tile).wait_recv()
        last = number == count
        low = 0 if last else features >> (number + 1)
        high = features >> number
        group = jnp.int32(0)
        for edge in edges:
            group = group + (tile >= edge).astype(jnp.int32)
        columns = pl.ds(pl.multiple_of(tile * width, width), width)
        each = right_ref.shape[2] // width
        own = pl.ds(pl.multiple_of(lax.rem(tile, each) * width, width), width)
        total = jnp.dot(
            held[plan, group, low:high],
            right_ref[tile // each, :, own],
            preferred_element_type=jnp.float32,
        )
        for earlier in range(number):
            total = total + got[earlier][slot, low:high].astype(jnp.float32)
        if last:
            out_ref[:, columns] = total

            @pl.when(tile < tiles - slots)
            def _():
                for step in range(count):
                    pl.semaphore_signal(
                        credit.at[plan, step],
                        inc=1,
                        device_id=partner_of(step, plan),
                        device_id_type=MESH,
                    )

            return

        @pl.when(tile >= 2)
        def _():
            transfer(number, tile - 2).wait_send()

        sent[number][lax.rem(tile, 2)] = total.astype(jnp.bfloat16)

        @pl.when(tile >= slots)
        def _():
            pl.semaphore_wait(credit.at[plan, number], 1)

        transfer(number, tile).start()

    def turn(index):
        for number in range(count + 1):
            tile = index - lags[number]

            @pl.when((tile >= 0) & (tile < tiles))
            def _(number=number, tile=tile):
                stage(number, tile)

    def finish():
        for step in range(count):
            for tile in range(max(0, tiles - 2), tiles):
                transfer(step, jnp.int32(tile)).wait_send()

    return loads, turn, finish, partners[0]


def greet(partners):
    barrier = pltpu.get_barrier_semaphore()
    for partner in partners:
        pl.semaphore_signal(barrier, inc=1, device_id=partner, device_id_type=MESH)
    pl.semaphore_wait(barrier, len(partners))


def fold_kernel(fold, lefts, *refs):
    left_refs, right_ref, out_ref, scratch = refs[:lefts], refs[lefts], refs[lefts + 1], refs[lefts + 2 :]
    loads, turn, finish, partners = fold_engine(*fold, left_refs, right_ref, out_ref, scratch)
    for load in loads:
        load.start()
    greet(partners)
    for load in loads:
        load.wait()

    def body(index, carry):
        turn(index)
        return carry

    lax.fori_loop(0, fold[2] + fold[6][-1], body, 0)
    finish()


def fold_lags(count):
    return (0,) + tuple(range(1, 2 * count, 2))


def fold_scratch(plans, lefts, features, rows, width, slots):
    count = len(plans[0])
    sizes = [features >> (step + 1) for step in range(count)]
    return [
        pltpu.VMEM((len(plans), lefts, features, rows), jnp.bfloat16),
        pltpu.SemaphoreType.DMA((len(plans), lefts, 1 << count)),
        pltpu.SemaphoreType.DMA((count, 2)),
        pltpu.SemaphoreType.DMA((count, slots)),
        pltpu.SemaphoreType.REGULAR((len(plans), count)),
        *[pltpu.VMEM((2, size, width), jnp.bfloat16) for size in sizes],
        *[pltpu.VMEM((slots, size, width), jnp.bfloat16) for size in sizes],
    ]


def fold_layout(lefts, right_sets, width, slots, period):
    steps = fold_steps()
    plans = [steps]
    if lax.axis_size("dp") > 2 and period and slots % period == 0:
        plans.append(late_steps(steps))
    edges, tiles = [], 0
    for many in right_sets:
        tiles += sum(right.shape[1] for right in many) // width
        edges.append(tiles)
    fold = (plans, edges[:-1], tiles, width, slots, period, fold_lags(len(steps)))
    features, rows = lefts[0].shape
    shape = jax.ShapeDtypeStruct((features >> len(steps), tiles * width), jnp.float32)
    scratch = fold_scratch(plans, len(lefts), features, rows, width, slots)
    cost = pl.CostEstimate(
        flops=2 * features * rows * tiles * width,
        bytes_accessed=tiles * width * features * 8,
        transcendentals=0,
    )
    return fold, shape, scratch, cost


def fold_setting(groups, width, slots, period):
    lefts = [left for left, _ in groups]
    right_sets = [many for _, many in groups]
    rights = jnp.concatenate([right for many in right_sets for right in many], axis=1)[None]
    fold, shape, scratch, cost = fold_layout(lefts, right_sets, width, slots, period)
    return fold, lefts, rights, shape, scratch, cost


def remote_params(call):
    return pltpu.CompilerParams(
        collective_id=call, has_side_effects=True, vmem_limit_bytes=63 * 1024 * 1024
    )


def fold_products(groups, call, width=256, slots=12, period=6):
    fold, lefts, rights, shape, scratch, cost = fold_setting(groups, width, slots, period)
    folded = pl.pallas_call(
        functools.partial(fold_kernel, fold, len(lefts)),
        out_shape=shape,
        in_specs=[pl.BlockSpec(memory_space=pl.ANY)] * len(lefts)
        + [pl.BlockSpec(memory_space=pltpu.VMEM)],
        out_specs=pl.BlockSpec(memory_space=pltpu.VMEM),
        scratch_shapes=scratch,
        compiler_params=remote_params(call),
        cost_estimate=cost,
    )(*lefts, rights)
    return unstacked(groups, folded)


def unstacked(groups, folded):
    shares, at = [], 0
    for _, many in groups:
        shares.append([])
        for right in many:
            shares[-1].append(folded[:, at : at + right.shape[1]])
            at += right.shape[1]
    return shares


def together(*arrays):
    return lax.optimization_barrier(arrays)


def fold_vector(vector):
    steps = fold_steps()
    offsets, part = fold_order(vector.shape[-1], steps)
    held = jnp.stack(
        [lax.dynamic_slice_in_dim(vector, offset, part, axis=-1) for offset in offsets], axis=0
    )
    for axis, bit in steps:
        half = held.shape[0] // 2
        held = held[:half] + swap(held[half:], axis, bit)
    return held[0]


def to_heads(pieces, blocks):
    rows, width = pieces[0].shape
    part = width // blocks
    packed = jnp.stack(
        [
            jnp.concatenate([piece[:, i * part : (i + 1) * part] for piece in pieces], axis=1)
            for i in range(blocks)
        ],
        axis=0,
    )
    moved = lax.all_to_all(packed, "blk", 0, 0)
    return moved.reshape(rows * blocks, part * len(pieces))


def swap_blocks(packed, blocks):
    length, columns = packed.shape
    return lax.all_to_all(packed.reshape(blocks, length // blocks, columns), "blk", 0, 0)


def side_by_side(moved, count):
    part = moved.shape[2] // count
    return [
        jnp.concatenate(
            [moved[j, :, i * part : (i + 1) * part] for j in range(moved.shape[0])], axis=1
        )
        for i in range(count)
    ]


def first_allowed(doc_ends, positions):
    first = jnp.zeros(positions.shape, jnp.int32)
    for number in range(doc_ends.shape[0]):
        end = doc_ends[number]
        first = jnp.maximum(first, jnp.where(end <= positions, end, 0))
    return first


def tile_probs(ends, packed, part, head, start, stop, factor):
    own = slice(head * HEAD, (head + 1) * HEAD)
    keys = packed[:stop, part + own.start : part + own.stop]
    scores = dot_rows(packed[start:stop, own], keys) * factor
    positions = start + lax.broadcasted_iota(jnp.int32, (stop - start, 1), 0)
    first = first_allowed(ends, positions)
    key_pos = lax.broadcasted_iota(jnp.int32, scores.shape, 1)
    allowed = (key_pos >= first) & (key_pos <= positions)
    scores = jnp.where(allowed, scores, NEGATIVE)
    weights = jnp.exp(scores - jnp.max(scores, axis=-1, keepdims=True))
    return weights / jnp.sum(weights, axis=-1, keepdims=True)


def attend_kernel(part, tile, factor, ends, packed, out):
    for head in range(part // HEAD):
        own = slice(head * HEAD, (head + 1) * HEAD)
        for start in range(0, packed.shape[0], tile):
            stop = start + tile
            probs = tile_probs(ends, packed, part, head, start, stop, factor)
            values = packed[:stop, 2 * part + own.start : 2 * part + own.stop]
            out[start:stop, own] = plain_dot(probs.astype(jnp.bfloat16), values).astype(out.dtype)


def attend_back_head(part, tile, factor, head, ends, packed, grads, out, key_sum, value_sum):
    length = packed.shape[0]
    own = slice(head * HEAD, (head + 1) * HEAD)
    key_own = slice(part + own.start, part + own.stop)
    value_own = slice(2 * part + own.start, 2 * part + own.stop)
    for start in reversed(range(0, length, tile)):
        stop = start + tile
        probs = tile_probs(ends, packed, part, head, start, stop, factor)
        grad = grads[start:stop, own]
        prob_grad = dot_rows(grad, packed[:stop, value_own])
        delta = jnp.sum(probs * prob_grad, axis=-1, keepdims=True)
        score_grad = (probs * (prob_grad - delta)).astype(jnp.bfloat16)
        query_grad = plain_dot(score_grad, packed[:stop, key_own]) * factor
        out[start:stop, own] = query_grad.astype(out.dtype)
        key_part = dot_cols(score_grad, packed[start:stop, own])
        value_part = dot_cols(probs.astype(jnp.bfloat16), grad)
        if stop == length:
            key_sum[:stop] = key_part
            value_sum[:stop] = value_part
        else:
            key_sum[:stop] += key_part
            value_sum[:stop] += value_part
    out[:, key_own] = (key_sum[...] * factor).astype(out.dtype)
    out[:, value_own] = value_sum[...].astype(out.dtype)


def attention_tile(length):
    return next(tile for tile in (512, 384, 256, 128, 64, 32, 16) if length % tile == 0)


def attention_call(kernel, doc_ends, arrays, columns, scratch, matmuls):
    length, width = arrays[0].shape
    part = width // 3
    tile = attention_tile(length)
    vmem = pl.BlockSpec(memory_space=pltpu.VMEM)
    return pl.pallas_call(
        functools.partial(kernel, part, tile, 1.0 / math.sqrt(HEAD)),
        out_shape=jax.ShapeDtypeStruct((length, columns), jnp.bfloat16),
        in_specs=[pl.BlockSpec(memory_space=pltpu.SMEM)] + [vmem] * len(arrays),
        out_specs=vmem,
        scratch_shapes=scratch,
        compiler_params=pltpu.CompilerParams(vmem_limit_bytes=48 * 1024 * 1024),
        cost_estimate=pl.CostEstimate(
            flops=2 * matmuls * length * length * part,
            bytes_accessed=10 * length * width,
            transcendentals=length * length * part // HEAD,
        ),
    )(doc_ends, *arrays)


def attend(doc_ends, packed):
    return attention_call(attend_kernel, doc_ends, [packed], packed.shape[1] // 3, [], 2)


def middle_kernel(
    fold, marks, tile, factor, ends, first_left, second_left, right_ref, attended_ref, cot_ref, gain_ref,
    weight_ref, packed_ref, mid, feed_ref, out_ref, resid_ref, gain_out, moved, result, *scratch
):
    count = len(fold[0][0])
    attended, cot, weight, packed, load_sem = scratch[:5]
    other, sent_grads, grads, out, key_sum, value_sum = scratch[5:11]
    heads_sem, ctx_sem, out_sem, strip_rows, strip_sem, ready = scratch[11:17]
    left_refs = (first_left, second_left)
    loads, turn, finish, partners = fold_engine(*fold, left_refs, right_ref, out_ref, scratch[17:])
    rows, features = mid.shape
    blocks, _, part = sent_grads.shape
    dp, blk, heads = (lax.axis_index(axis) for axis in MESH_AXES)

    def away(distance):
        at, bit = blk, 1
        while bit <= distance:
            if distance & bit:
                at = flipped(at, bit)
            bit *= 2
        return at

    mirror = (dp, blk, flipped(heads, 1))
    met = partners + [mirror]
    met += [(dp, away(d), heads) for d in range(1, blocks) if d & (d - 1)]
    loads = loads + [
        pltpu.make_async_copy(source, target, load_sem.at[number])
        for number, (source, target) in enumerate(
            [(attended_ref, attended), (cot_ref, cot), (weight_ref, weight), (packed_ref, packed)]
        )
    ]
    for load in loads:
        load.start()
    strip = strip_rows.shape[1]
    strips = features // strip
    units = right_ref.shape[2]

    def strip_copy(number):
        slot = lax.rem(number, 2)
        rows_of = pl.ds(pl.multiple_of(number * strip, strip), strip)
        return pltpu.make_async_copy(
            feed_ref.at[rows_of, pl.ds(2 * units, units)], strip_rows.at[slot], strip_sem.at[slot]
        )

    def strip_step(number):
        strip_copy(number).wait()

        @pl.when(number + 1 < strips)
        def _():
            strip_copy(number + 1).start()

        columns = pl.ds(pl.multiple_of(number * strip, strip), strip)
        product = dot_rows(right_ref[2], strip_rows[lax.rem(number, 2)])
        cot[:, columns] = product.astype(jnp.bfloat16)

    greet(met)

    def mirrored(source, number):
        return pltpu.make_async_remote_copy(
            src_ref=source,
            dst_ref=other,
            send_sem=heads_sem.at[0, number],
            recv_sem=heads_sem.at[1, number],
            device_id=mirror,
            device_id_type=MESH,
        )

    first, second = mirrored(mid, 0), mirrored(cot, 1)
    first.start()
    for load in loads:
        load.wait()

    def block(index):
        return pl.ds(pl.multiple_of(index * rows, rows), rows)

    def ctx_copy(distance, landing):
        return pltpu.make_async_remote_copy(
            src_ref=sent_grads.at[away(distance)],
            dst_ref=grads.at[block(landing)],
            send_sem=ctx_sem.at[0, distance],
            recv_sem=ctx_sem.at[1, distance],
            device_id=(dp, away(distance), heads),
            device_id_type=MESH,
        )

    def landing_of(kind, source):
        offset = kind * (part * blocks) + source * part
        return moved.at[:, pl.ds(pl.multiple_of(offset, part), part)]

    def out_copy(kind, distance, landing):
        return pltpu.make_async_remote_copy(
            src_ref=out.at[block(away(distance)), pl.ds(kind * part, part)],
            dst_ref=landing_of(kind, landing),
            send_sem=out_sem.at[0, kind, distance],
            recv_sem=out_sem.at[1, kind, distance],
            device_id=(dp, away(distance), heads),
            device_id_type=MESH,
        )

    step = rows // 3 if rows % 48 == 0 else rows
    starts = list(range(0, rows, step))

    def norm_back(start):
        if start == 0:
            first.wait()
        for start in (start,):
            own = slice(start, start + step)
            values = attended[own]
            mid_grad = pair_add(mid[own], other[own])
            scale = lax.rsqrt(jnp.mean(values * values, axis=-1, keepdims=True) + EPSILON)
            normed = values * scale
            scaled = mid_grad * gain_ref[...]
            inner = jnp.mean(scaled * normed, axis=-1, keepdims=True)
            total = cot[own].astype(jnp.float32) + scale * (scaled - normed * inner)
            resid_ref[own] = total
            gain_part = jnp.sum(mid_grad * normed, axis=0, keepdims=True)
            if start == 0:
                gain_out[...] = gain_part
            else:
                gain_out[...] += gain_part
            low = plain_dot(total.astype(jnp.bfloat16), weight[...]).astype(jnp.bfloat16)
            for number in range(blocks):
                sent_grads[number, own] = low[:, number * part : (number + 1) * part]
        if start != starts[-1]:
            return
        grads[block(blk)] = sent_grads[blk]
        for distance in range(1, blocks):
            ctx_copy(distance, blk).start()

    def one_head(head):
        attend_back_head(part, tile, factor, head, ends, packed, grads, out, key_sum, value_sum)

    def body(index, carry):
        turn(index)

        for number, start in enumerate(starts):

            @pl.when(index == marks[0] + number)
            def _(start=start):
                norm_back(start)

        done = marks[0] + len(starts) - 1

        @pl.when(index == done)
        def _():
            pl.semaphore_signal(ready, inc=1, device_id=mirror, device_id_type=MESH)
            strip_copy(jnp.int32(0)).start()

        @pl.when((index > done) & (index <= done + strips))
        def _():
            strip_step(index - done - 1)

        @pl.when(index == done + strips)
        def _():
            pl.semaphore_wait(ready, 1)
            second.start()

        @pl.when(index == marks[1])
        def _():
            for distance in range(1, blocks):
                ctx_copy(distance, away(distance)).wait_recv()
                ctx_copy(distance, blk).wait_send()

        for head in range(part // HEAD):

            @pl.when(index == marks[1] + head)
            def _(head=head):
                one_head(head)

        @pl.when(index == marks[1] + part // HEAD - 1)
        def _():
            for kind in range(3):
                offset = pl.multiple_of(kind * (part * blocks) + blk * part, part)
                moved[:, pl.ds(offset, part)] = out[block(blk), kind * part : (kind + 1) * part]

        for number in range(3 * (blocks - 1)):

            @pl.when(index == marks[1] + part // HEAD + 2 * number)
            def _(kind=number // (blocks - 1), distance=number % (blocks - 1) + 1):
                out_copy(kind, distance, blk).start()

        return carry

    lax.fori_loop(0, fold[2] + fold[6][-1], body, 0)
    finish()
    second.wait()
    for start in starts:
        own = slice(start, start + step)
        result[own] = (attended[own] + pair_add(cot[own], other[own])).astype(result.dtype)
    for kind in range(3):
        for distance in range(1, blocks):
            out_copy(kind, distance, away(distance)).wait_recv()
            out_copy(kind, distance, blk).wait_send()


def middle(lefts, rights, doc_ends, attended, cot, gain, weight, packed, mid, feed, call, marks, width=256, slots=10):
    each = rights.shape[2]
    sizes = [jax.ShapeDtypeStruct((1, each), jnp.bfloat16)] * 3
    fold, shape, scratch, cost = fold_layout(lefts, [sizes[:2], sizes[2:]], width, slots, 0)
    blocks = lax.axis_size("blk")
    rows, features = attended.shape
    length, columns = packed.shape
    part = columns // 3
    tile = 256 if length % 256 == 0 else attention_tile(length)
    turns = fold[2] + fold[6][-1]
    assert marks[0] + 3 + STRIPS < turns and marks[0] < marks[1] - 3
    assert marks[1] + part // HEAD + 2 * 3 * (blocks - 1) < turns
    vmem, anywhere = (pl.BlockSpec(memory_space=space) for space in (pltpu.VMEM, pl.ANY))
    low = jnp.bfloat16
    folded, resid, gain_grad, moved, result = pl.pallas_call(
        functools.partial(middle_kernel, fold, marks, tile, 1.0 / math.sqrt(HEAD)),
        out_shape=(
            shape,
            jax.ShapeDtypeStruct(attended.shape, jnp.float32),
            jax.ShapeDtypeStruct((1, features), jnp.float32),
            jax.ShapeDtypeStruct((rows, columns * blocks), low),
            jax.ShapeDtypeStruct((rows, features), low),
        ),
        in_specs=[
            pl.BlockSpec(memory_space=pltpu.SMEM),
            anywhere,
            anywhere,
            vmem,
            anywhere,
            anywhere,
            vmem,
            anywhere,
            anywhere,
            vmem,
            anywhere,
        ],
        out_specs=(vmem,) * 5,
        scratch_shapes=[
            pltpu.VMEM(attended.shape, jnp.float32),
            pltpu.VMEM(cot.shape, low),
            pltpu.VMEM(weight.shape, low),
            pltpu.VMEM(packed.shape, low),
            pltpu.SemaphoreType.DMA((4,)),
            pltpu.VMEM(cot.shape, low),
            pltpu.VMEM((blocks, rows, part), low),
            pltpu.VMEM((length, part), low),
            pltpu.VMEM((length, columns), low),
            pltpu.VMEM((length, HEAD), jnp.float32),
            pltpu.VMEM((length, HEAD), jnp.float32),
            pltpu.SemaphoreType.DMA((2, 2)),
            pltpu.SemaphoreType.DMA((2, blocks)),
            pltpu.SemaphoreType.DMA((2, 3, blocks)),
            pltpu.VMEM((2, features // STRIPS, each), low),
            pltpu.SemaphoreType.DMA((2,)),
            pltpu.SemaphoreType.REGULAR,
            *scratch,
        ],
        compiler_params=remote_params(call),
        cost_estimate=cost,
    )(doc_ends, *lefts, rights, attended, cot, gain[None], weight, packed, mid, feed)
    shares = [folded[:, number * each : (number + 1) * each] for number in range(3)]
    return shares, resid, gain_grad[0], moved, result


def last_kernel(
    fold, marks, first_left, second_left, third_left, right_ref, normed_part, memory_part, hidden_ref,
    memory_ref, resid_ref, gains_ref, mid_gain_ref, out_ref, hidden_grad, memory_grad, gain_out, *scratch
):
    steps = fold[0][0]
    count = len(steps)
    normed_other, memory_other, hidden, memory, resid = scratch[:5]
    load_sem, heads_sem, gain_sem, gain_held = scratch[5:9]
    gain_got = scratch[9 : 9 + count]
    left_refs = (first_left, second_left, third_left)
    loads, turn, finish, partners = fold_engine(
        *fold, left_refs, right_ref, out_ref, scratch[9 + count :]
    )
    rows, features = normed_part.shape
    dp, blk, heads = (lax.axis_index(axis) for axis in MESH_AXES)
    mirror = (dp, blk, flipped(heads, 1))
    loads = loads + [
        pltpu.make_async_copy(source, target, load_sem.at[number])
        for number, (source, target) in enumerate(
            [(hidden_ref, hidden), (memory_ref, memory), (resid_ref, resid)]
        )
    ]
    for load in loads:
        load.start()
    greet(partners + [mirror])
    mirrored = [
        pltpu.make_async_remote_copy(
            src_ref=source,
            dst_ref=target,
            send_sem=heads_sem.at[0, number],
            recv_sem=heads_sem.at[1, number],
            device_id=mirror,
            device_id_type=MESH,
        )
        for number, (source, target) in enumerate(
            [(normed_part, normed_other), (memory_part, memory_other)]
        )
    ]
    for copy in mirrored:
        copy.start()
    for load in loads:
        load.wait()
    offsets, part = fold_order(features, steps)

    def keep_gain(number, gain_grad):
        for place, offset in enumerate(offsets):
            columns = pl.ds(pl.multiple_of(offset, part), part)
            gain_held[place, number : number + 1] = gain_grad[:, columns]

    def norm_back(number):
        mirrored[number].wait()
        own, other = ((normed_part, normed_other), (memory_part, memory_other))[number]
        source, target = ((hidden, hidden_grad), (memory, memory_grad))[number]
        step = rows // 3 if rows % 48 == 0 else rows
        gain_total = None
        for start in range(0, rows, step):
            here = slice(start, start + step)
            values = source[here].astype(jnp.float32)
            grad = pair_add(own[here], other[here])
            scale = lax.rsqrt(jnp.mean(values * values, axis=-1, keepdims=True) + EPSILON)
            normed = values * scale
            scaled = grad * gains_ref[number : number + 1]
            inner = jnp.mean(scaled * normed, axis=-1, keepdims=True)
            total = scale * (scaled - normed * inner)
            target[here] = total + resid[here] if number == 0 else total
            gain_part = jnp.sum(grad * normed, axis=0, keepdims=True)
            gain_total = gain_part if gain_total is None else gain_total + gain_part
        gain_sum[...] = gain_total
        keep_gain(number, gain_sum)

    gain_sum = scratch[-1]

    def gain_copy(step):
        half = (1 << count) >> (step + 1)
        return pltpu.make_async_remote_copy(
            src_ref=gain_held.at[pl.ds(half, half)],
            dst_ref=gain_got[step],
            send_sem=gain_sem.at[0, step],
            recv_sem=gain_sem.at[1, step],
            device_id=partners[step],
            device_id_type=MESH,
        )

    def gain_step(step):
        if step > 0:
            gain_copy(step - 1).wait()
            half = (1 << count) >> step
            gain_held[:half] += gain_got[step - 1][...]
        if step < count:
            gain_copy(step).start()

    def body(index, carry):
        turn(index)

        @pl.when(index == marks[0])
        def _():
            gain_held[...] = jnp.zeros_like(gain_held)
            keep_gain(2, mid_gain_ref)
            norm_back(0)

        @pl.when(index == marks[1])
        def _():
            norm_back(1)

        for step in range(count):

            @pl.when(index == marks[1] + step)
            def _(step=step):
                gain_step(step)

        return carry

    lax.fori_loop(0, fold[2] + fold[6][-1], body, 0)
    gain_step(count)
    gain_out[...] = gain_held[0]
    finish()


def last(groups, normed_part, memory_part, hidden, memory, resid, gains, mid_gain_grad, call, marks, width=256, slots=12):
    fold, lefts, rights, shape, scratch, cost = fold_setting(groups, width, slots, 6)
    count = len(fold[0][0])
    marks = tuple(min(mark, fold[2] + fold[6][-1] - count) for mark in marks)
    rows, features = normed_part.shape
    part = features >> count
    vmem, anywhere = (pl.BlockSpec(memory_space=space) for space in (pltpu.VMEM, pl.ANY))
    folded, hidden_grad, memory_grad, gain_grads = pl.pallas_call(
        functools.partial(last_kernel, fold, marks),
        out_shape=(
            shape,
            jax.ShapeDtypeStruct(hidden.shape, jnp.float32),
            jax.ShapeDtypeStruct(hidden.shape, jnp.float32),
            jax.ShapeDtypeStruct((8, part), jnp.float32),
        ),
        in_specs=[anywhere] * 3 + [vmem] * 3 + [anywhere] * 3 + [vmem] * 2,
        out_specs=(vmem,) * 4,
        scratch_shapes=[
            pltpu.VMEM(hidden.shape, jnp.bfloat16),
            pltpu.VMEM(hidden.shape, jnp.bfloat16),
            pltpu.VMEM(hidden.shape, jnp.bfloat16),
            pltpu.VMEM(hidden.shape, jnp.bfloat16),
            pltpu.VMEM(hidden.shape, jnp.float32),
            pltpu.SemaphoreType.DMA((3,)),
            pltpu.SemaphoreType.DMA((2, 2)),
            pltpu.SemaphoreType.DMA((2, count)),
            pltpu.VMEM((1 << count, 8, part), jnp.float32),
            *[pltpu.VMEM(((1 << count) >> (step + 1), 8, part), jnp.float32) for step in range(count)],
            *scratch,
            pltpu.VMEM((1, features), jnp.float32),
        ],
        compiler_params=remote_params(call),
        cost_estimate=cost,
    )(*lefts, rights, normed_part, memory_part, hidden, memory, resid, gains, mid_gain_grad[None])
    return unstacked(groups, folded), hidden_grad, memory_grad, gain_grads


def feed_kernel(mid_ref, cot_ref, gate_ref, up_ref, down_ref, out_ref):
    gate = plain_dot(mid_ref[...], gate_ref[...])
    upward = plain_dot(mid_ref[...], up_ref[...])
    act_grad = plain_dot(cot_ref[...], down_ref[...])
    sigma = jax.nn.sigmoid(gate)
    silu_gate = gate * sigma
    gate_grad = act_grad * upward * sigma * (1.0 + gate * (1.0 - sigma))
    out_ref[0] = gate_grad.astype(jnp.bfloat16)
    out_ref[1] = (act_grad * silu_gate).astype(jnp.bfloat16)
    out_ref[2] = (silu_gate * upward).astype(jnp.bfloat16)


def feed(mid, cot, full, width=256):
    rows, features = mid.shape
    units = full.shape[1] // 3
    steps = units // width
    whole = pl.BlockSpec((rows, features), lambda i: (0, 0))
    return pl.pallas_call(
        feed_kernel,
        grid=(steps,),
        out_shape=jax.ShapeDtypeStruct((3, rows, units), jnp.bfloat16),
        in_specs=[whole, whole]
        + [
            pl.BlockSpec((features, width), lambda i, number=number: (0, number * steps + i))
            for number in range(3)
        ],
        out_specs=pl.BlockSpec((3, rows, width), lambda i: (0, 0, i)),
        compiler_params=pltpu.CompilerParams(vmem_limit_bytes=40 * 1024 * 1024),
        cost_estimate=pl.CostEstimate(
            flops=6 * rows * features * units,
            bytes_accessed=6 * features * units,
            transcendentals=rows * units,
        ),
    )(mid, cot, full, full, full)


def by_head(array):
    return array.reshape(array.shape[0], -1, HEAD).transpose(1, 0, 2)


def from_heads(array):
    return array.transpose(1, 0, 2).reshape(array.shape[1], -1).astype(jnp.bfloat16)


def plain_probs(doc_ends, query_pos, query, key):
    key_pos = jnp.arange(key.shape[0], dtype=jnp.int32)
    first = first_allowed(doc_ends, query_pos)
    allowed = (key_pos[None, :] >= first[:, None]) & (key_pos[None, :] <= query_pos[:, None])
    scores = dot_rows(query, key) * (1.0 / math.sqrt(HEAD))
    return jax.nn.softmax(jnp.where(allowed, scores, NEGATIVE), axis=-1)


def plain_attend(doc_ends, query_pos, queries, keys, values):
    def one(arrays):
        query, key, value = arrays
        probs = plain_probs(doc_ends, query_pos, query, key)
        return plain_dot(probs.astype(jnp.bfloat16), value)

    return from_heads(lax.map(one, (by_head(queries), by_head(keys), by_head(values))))


def plain_attend_back(doc_ends, query_pos, queries, keys, values, grads):
    factor = 1.0 / math.sqrt(HEAD)

    def one(arrays):
        query, key, value, grad = arrays
        probs = plain_probs(doc_ends, query_pos, query, key)
        prob_grad = dot_rows(grad, value)
        delta = jnp.sum(probs * prob_grad, axis=-1, keepdims=True)
        score_grad = (probs * (prob_grad - delta)).astype(jnp.bfloat16)
        return (
            plain_dot(score_grad, key) * factor,
            dot_cols(score_grad, query) * factor,
            dot_cols(probs.astype(jnp.bfloat16), grad),
        )

    arrays = tuple(by_head(array) for array in (queries, keys, values, grads))
    return tuple(from_heads(grad) for grad in lax.map(one, arrays))


def local(
    hidden_in,
    memory,
    lengths,
    query_weight,
    key_weight,
    value_weight,
    output_weight,
    gate_weight,
    up_weight,
    down_weight,
    attention_gain,
    memory_gain,
    feedforward_gain,
    cotangent,
):
    rows, features = hidden_in.shape
    blocks = lax.axis_size("blk")
    width = query_weight.shape[1]
    hidden_units = gate_weight.shape[1]
    heads_local = width // HEAD
    spread = heads_local % blocks == 0 and lax.axis_size("heads") == 2
    doc_ends = jnp.cumsum(lengths[0], dtype=jnp.int32)

    gains = jnp.stack([attention_gain, memory_gain, feedforward_gain], axis=1)
    gains = jnp.pad(gains, ((0, 0), (0, LANES - gains.shape[1])))
    attn_mine = jnp.concatenate(
        [query_weight, key_weight, value_weight, output_weight, gains], axis=1
    )
    attn_full = lax.all_gather(attn_mine, ("dp", "blk"), axis=0, tiled=True)
    padded = -(-hidden_units // (2 * LANES)) * (2 * LANES)
    ffn_mine = jnp.concatenate(
        [
            jnp.pad(weight, ((0, 0), (0, padded - hidden_units)))
            for weight in (gate_weight, up_weight, down_weight)
        ],
        axis=1,
    )
    ffn_mine, attn_full = together(ffn_mine, attn_full)
    ffn_full = lax.all_gather(ffn_mine, ("dp", "blk"), axis=0, tiled=True)

    full_query = attn_full[:, :width]
    full_key = attn_full[:, width : 2 * width]
    full_value = attn_full[:, 2 * width : 3 * width]
    full_output = attn_full[:, 3 * width : 4 * width]
    full_gains = attn_full[:, 4 * width : 4 * width + 3].astype(jnp.float32).T
    input_gain, source_gain, mid_gain = full_gains[0], full_gains[1], full_gains[2]

    hidden_float = hidden_in.astype(jnp.float32)
    memory_float = memory.astype(jnp.float32)
    memory_low = rms_scale(memory_float, source_gain).astype(jnp.bfloat16)
    normed_low = rms_scale(hidden_float, input_gain).astype(jnp.bfloat16)
    key_low = plain_dot(memory_low, full_key).astype(jnp.bfloat16)
    value_low = plain_dot(memory_low, full_value).astype(jnp.bfloat16)
    query_low = plain_dot(normed_low, full_query).astype(jnp.bfloat16)

    if spread:
        packed = to_heads([query_low, key_low, value_low], blocks)
        context_low = side_by_side(swap_blocks(attend(doc_ends, packed), blocks), 1)[0]
    else:
        query_pos = lax.axis_index("blk") * rows + jnp.arange(rows, dtype=jnp.int32)
        key_all = lax.all_gather(key_low, "blk", axis=0, tiled=True)
        value_all = lax.all_gather(value_low, "blk", axis=0, tiled=True)
        context_low = plain_attend(doc_ends, query_pos, query_low, key_all, value_all)

    attended = hidden_float + pair_sum(dot_rows(context_low, full_output))
    attended, cot_turned, normed_turned, memory_turned = together(
        attended, cotangent.T, normed_low.T, memory_low.T
    )
    mid_low = rms_scale(attended, mid_gain).astype(jnp.bfloat16)

    rights = feed(mid_low, cotangent, ffn_full)
    full_gate, full_up, full_down = (ffn_full[:, i * padded : (i + 1) * padded] for i in range(3))
    mid_part = dot_rows(rights[0], full_gate) + dot_rows(rights[1], full_up)
    mid_part = mid_part.astype(jnp.bfloat16)
    if spread:
        shares, attended_grad, mid_gain_grad, moved, output = middle(
            (mid_low.T, cot_turned),
            rights,
            doc_ends,
            attended,
            cotangent,
            mid_gain,
            full_output,
            packed,
            mid_part,
            ffn_full,
            0,
            MARKS,
        )
        resid_low = attended_grad.astype(jnp.bfloat16)
        query_grad_low, key_grad_low, value_grad_low = (
            moved[:, i * width : (i + 1) * width] for i in range(3)
        )
    else:
        gate_grad_low, up_grad_low, act_low = rights[0], rights[1], rights[2]
        shares = fold_products(
            [(mid_low.T, [gate_grad_low, up_grad_low]), (cot_turned, [act_low])], 0
        )
        shares = [*shares[0], *shares[1]]
        output = (attended + pair_sum(dot_rows(act_low, full_down))).astype(jnp.bfloat16)
        mid_grad = pair_sum(mid_part)
        attended_norm_grad, mid_gain_grad = jax.vjp(rms_scale, attended, mid_gain)[1](mid_grad)
        attended_grad = cotangent.astype(jnp.float32) + attended_norm_grad
        resid_low = attended_grad.astype(jnp.bfloat16)
        context_grad_low = plain_dot(resid_low, full_output).astype(jnp.bfloat16)
        query_grad_low, key_grad, value_grad = plain_attend_back(
            doc_ends, query_pos, query_low, key_all, value_all, context_grad_low
        )
        moved = lax.psum_scatter(
            jnp.concatenate([key_grad, value_grad], axis=1), "blk", scatter_dimension=0, tiled=True
        )
        key_grad_low, value_grad_low = moved[:, :width], moved[:, width:]
    gate_share, up_share, down_share = shares
    normed_part = dot_rows(query_grad_low, full_query).astype(jnp.bfloat16)
    memory_part = (
        dot_rows(key_grad_low, full_key) + dot_rows(value_grad_low, full_value)
    ).astype(jnp.bfloat16)
    if spread:
        right_sets = ([context_low], [moved[:, :width]], [moved[:, width:]])
    else:
        right_sets = ([context_low], [query_grad_low], [key_grad_low, value_grad_low])
    products = list(zip((resid_low.T, normed_turned, memory_turned), right_sets))
    if spread:
        shares, hidden_grad, memory_grad, gain_shares = last(
            products,
            normed_part,
            memory_part,
            hidden_in,
            memory,
            attended_grad,
            jnp.stack([input_gain, source_gain], axis=0),
            mid_gain_grad,
            1,
            LAST_MARKS,
        )
    else:
        shares = fold_products(products, 1)
        normed_grad = pair_sum(normed_part)
        memory_in_grad = pair_sum(memory_part)
        hidden_norm_grad, input_gain_grad = jax.vjp(rms_scale, hidden_float, input_gain)[1](
            normed_grad
        )
        memory_grad, source_gain_grad = jax.vjp(rms_scale, memory_float, source_gain)[1](
            memory_in_grad
        )
        hidden_grad = attended_grad + hidden_norm_grad
        gain_shares = fold_vector(
            jnp.stack([input_gain_grad, source_gain_grad, mid_gain_grad], axis=0)
        )
    (output_share,), (query_share,), both = shares
    both = jnp.concatenate(both, axis=1)
    key_share, value_share = both[:, :width], both[:, width:]
    gate_share, up_share, down_share = (
        share[:, :hidden_units] for share in (gate_share, up_share, down_share)
    )
    return (
        output,
        hidden_grad,
        memory_grad,
        query_share,
        key_share,
        value_share,
        output_share,
        gate_share,
        up_share,
        down_share,
        gain_shares[0],
        gain_shares[1],
        gain_shares[2],
    )


def solution(mesh):
    tokens = P(("dp", "blk"), None)
    weight = P(("dp", "blk"), "heads")
    gain = P(("dp", "blk"))
    return jax.shard_map(
        local,
        mesh=mesh,
        in_specs=(tokens, tokens, P("dp", None)) + (weight,) * 7 + (gain,) * 3 + (tokens,),
        out_specs=(tokens,) * 3 + (weight,) * 7 + (gain,) * 3,
        check_vma=False,
    )
```

```python
import functools
import math

import jax
import jax.numpy as jnp
from jax import lax
from jax.experimental import pallas as pl
from jax.experimental.pallas import tpu as pltpu
from jax.sharding import PartitionSpec as P

MESH = pl.DeviceIdType.MESH
HEAD = 128
LANES = 128
MARKS = (7, 13)
STRIPS = 16
LAST_MARKS = (8, 15)
MESH_AXES = ("dp", "blk", "heads")
EPSILON = 1e-06
NEGATIVE = -1e30


def rms_scale(values, gain):
    return values * lax.rsqrt(jnp.mean(values * values, axis=-1, keepdims=True) + EPSILON) * gain


def plain_dot(left, right):
    return jnp.dot(left, right, preferred_element_type=jnp.float32)


def dot_rows(left, right):
    return lax.dot_general(
        left, right, (((1,), (1,)), ((), ())), preferred_element_type=jnp.float32
    )


def dot_cols(left, right):
    return lax.dot_general(
        left, right, (((0,), (0,)), ((), ())), preferred_element_type=jnp.float32
    )


def swap(array, axis, bit):
    size = lax.axis_size(axis)
    return lax.ppermute(array, axis, [(i, i ^ bit) for i in range(size)])


def heads_other(low):
    if lax.axis_size("heads") == 2:
        return swap(low, "heads", 1)
    return (lax.psum(low.astype(jnp.float32), "heads") - low.astype(jnp.float32)).astype(low.dtype)


def pair_add(low, other):
    return low.astype(jnp.float32) + other.astype(jnp.float32)


def pair_sum(part):
    low = part.astype(jnp.bfloat16)
    return pair_add(low, heads_other(low))


def fold_steps():
    steps = []
    for axis in ("dp", "blk"):
        size, bit = lax.axis_size(axis), 1
        while bit < size:
            steps.append((axis, bit))
            bit *= 2
    return steps


def late_steps(steps):
    first = [step for step in steps if step[0] == "dp"][1:]
    return [step for step in steps if step not in first] + first


def fold_order(width, steps):
    shards = 2 ** len(steps)
    part = width // shards
    offsets = []
    for place in range(shards):
        at = {axis: lax.axis_index(axis) for axis in ("dp", "blk")}
        for number, (axis, bit) in enumerate(steps):
            if place >> (len(steps) - 1 - number) & 1:
                at[axis] = flipped(at[axis], bit)
        offsets.append((at["dp"] * lax.axis_size("blk") + at["blk"]) * part)
    return offsets, part


def flipped(index, bit):
    return index + bit * (1 - 2 * ((index // bit) % 2))


def fold_engine(plans, edges, tiles, width, slots, period, lags, left_refs, right_ref, out_ref, scratch):
    count = len(plans[0])
    held, load_sem, send_sem, recv_sem, credit = scratch[:5]
    sent, got = scratch[5 : 5 + count], scratch[5 + count : 5 + 2 * count]
    lefts, features = held.shape[1:3]
    here = [lax.axis_index(axis) for axis in MESH_AXES]
    partners = [
        [
            tuple(
                flipped(place, bit) if name == axis else place
                for name, place in zip(MESH_AXES, here)
            )
            for axis, bit in steps
        ]
        for steps in plans
    ]
    loads = []
    for plan, steps in enumerate(plans):
        offsets, part = fold_order(features, steps)
        for number in range(lefts):
            for place, offset in enumerate(offsets):
                loads.append(
                    pltpu.make_async_copy(
                        left_refs[number].at[pl.ds(pl.multiple_of(offset, part), part)],
                        held.at[plan, number, pl.ds(place * part, part)],
                        load_sem.at[plan, number, place],
                    )
                )

    def plan_of(tile):
        return jnp.where(lax.rem(tile, period) == period - 1, 1, 0) if len(plans) > 1 else 0

    def partner_of(step, plan):
        if len(plans) == 1:
            return partners[0][step]
        return tuple(
            usual + plan * (other - usual)
            for usual, other in zip(partners[0][step], partners[1][step])
        )

    def transfer(step, tile):
        return pltpu.make_async_remote_copy(
            src_ref=sent[step].at[lax.rem(tile, 2)],
            dst_ref=got[step].at[lax.rem(tile, slots)],
            send_sem=send_sem.at[step, lax.rem(tile, 2)],
            recv_sem=recv_sem.at[step, lax.rem(tile, slots)],
            device_id=partner_of(step, plan_of(tile)),
            device_id_type=MESH,
        )

    def stage(number, tile):
        slot = lax.rem(tile, slots)
        plan = plan_of(tile)
        if number > 0:
            transfer(number - 1, tile).wait_recv()
        last = number == count
        low = 0 if last else features >> (number + 1)
        high = features >> number
        group = jnp.int32(0)
        for edge in edges:
            group = group + (tile >= edge).astype(jnp.int32)
        columns = pl.ds(pl.multiple_of(tile * width, width), width)
        each = right_ref.shape[2] // width
        own = pl.ds(pl.multiple_of(lax.rem(tile, each) * width, width), width)
        total = jnp.dot(
            held[plan, group, low:high],
            right_ref[tile // each, :, own],
            preferred_element_type=jnp.float32,
        )
        for earlier in range(number):
            total = total + got[earlier][slot, low:high].astype(jnp.float32)
        if last:
            out_ref[:, columns] = total

            @pl.when(tile < tiles - slots)
            def _():
                for step in range(count):
                    pl.semaphore_signal(
                        credit.at[plan, step],
                        inc=1,
                        device_id=partner_of(step, plan),
                        device_id_type=MESH,
                    )

            return

        @pl.when(tile >= 2)
        def _():
            transfer(number, tile - 2).wait_send()

        sent[number][lax.rem(tile, 2)] = total.astype(jnp.bfloat16)

        @pl.when(tile >= slots)
        def _():
            pl.semaphore_wait(credit.at[plan, number], 1)

        transfer(number, tile).start()

    def turn(index):
        for number in range(count + 1):
            tile = index - lags[number]

            @pl.when((tile >= 0) & (tile < tiles))
            def _(number=number, tile=tile):
                stage(number, tile)

    def finish():
        for step in range(count):
            for tile in range(max(0, tiles - 2), tiles):
                transfer(step, jnp.int32(tile)).wait_send()

    return loads, turn, finish, partners[0]


def greet(partners):
    barrier = pltpu.get_barrier_semaphore()
    for partner in partners:
        pl.semaphore_signal(barrier, inc=1, device_id=partner, device_id_type=MESH)
    pl.semaphore_wait(barrier, len(partners))


def fold_kernel(fold, lefts, *refs):
    left_refs, right_ref, out_ref, scratch = refs[:lefts], refs[lefts], refs[lefts + 1], refs[lefts + 2 :]
    loads, turn, finish, partners = fold_engine(*fold, left_refs, right_ref, out_ref, scratch)
    for load in loads:
        load.start()
    greet(partners)
    for load in loads:
        load.wait()

    def body(index, carry):
        turn(index)
        return carry

    lax.fori_loop(0, fold[2] + fold[6][-1], body, 0)
    finish()


def fold_lags(count):
    return (0,) + tuple(range(1, 2 * count, 2))


def fold_scratch(plans, lefts, features, rows, width, slots):
    count = len(plans[0])
    sizes = [features >> (step + 1) for step in range(count)]
    return [
        pltpu.VMEM((len(plans), lefts, features, rows), jnp.bfloat16),
        pltpu.SemaphoreType.DMA((len(plans), lefts, 1 << count)),
        pltpu.SemaphoreType.DMA((count, 2)),
        pltpu.SemaphoreType.DMA((count, slots)),
        pltpu.SemaphoreType.REGULAR((len(plans), count)),
        *[pltpu.VMEM((2, size, width), jnp.bfloat16) for size in sizes],
        *[pltpu.VMEM((slots, size, width), jnp.bfloat16) for size in sizes],
    ]


def fold_layout(lefts, right_sets, width, slots, period):
    steps = fold_steps()
    plans = [steps]
    if lax.axis_size("dp") > 2 and period and slots % period == 0:
        plans.append(late_steps(steps))
    edges, tiles = [], 0
    for many in right_sets:
        tiles += sum(right.shape[1] for right in many) // width
        edges.append(tiles)
    fold = (plans, edges[:-1], tiles, width, slots, period, fold_lags(len(steps)))
    features, rows = lefts[0].shape
    shape = jax.ShapeDtypeStruct((features >> len(steps), tiles * width), jnp.float32)
    scratch = fold_scratch(plans, len(lefts), features, rows, width, slots)
    cost = pl.CostEstimate(
        flops=2 * features * rows * tiles * width,
        bytes_accessed=tiles * width * features * 8,
        transcendentals=0,
    )
    return fold, shape, scratch, cost


def fold_setting(groups, width, slots, period):
    lefts = [left for left, _ in groups]
    right_sets = [many for _, many in groups]
    rights = jnp.concatenate([right for many in right_sets for right in many], axis=1)[None]
    fold, shape, scratch, cost = fold_layout(lefts, right_sets, width, slots, period)
    return fold, lefts, rights, shape, scratch, cost


def remote_params(call):
    return pltpu.CompilerParams(
        collective_id=call, has_side_effects=True, vmem_limit_bytes=63 * 1024 * 1024
    )


def fold_products(groups, call, width=256, slots=12, period=6):
    fold, lefts, rights, shape, scratch, cost = fold_setting(groups, width, slots, period)
    folded = pl.pallas_call(
        functools.partial(fold_kernel, fold, len(lefts)),
        out_shape=shape,
        in_specs=[pl.BlockSpec(memory_space=pl.ANY)] * len(lefts)
        + [pl.BlockSpec(memory_space=pltpu.VMEM)],
        out_specs=pl.BlockSpec(memory_space=pltpu.VMEM),
        scratch_shapes=scratch,
        compiler_params=remote_params(call),
        cost_estimate=cost,
    )(*lefts, rights)
    return unstacked(groups, folded)


def unstacked(groups, folded):
    shares, at = [], 0
    for _, many in groups:
        shares.append([])
        for right in many:
            shares[-1].append(folded[:, at : at + right.shape[1]])
            at += right.shape[1]
    return shares


def together(*arrays):
    return lax.optimization_barrier(arrays)


def fold_vector(vector):
    steps = fold_steps()
    offsets, part = fold_order(vector.shape[-1], steps)
    held = jnp.stack(
        [lax.dynamic_slice_in_dim(vector, offset, part, axis=-1) for offset in offsets], axis=0
    )
    for axis, bit in steps:
        half = held.shape[0] // 2
        held = held[:half] + swap(held[half:], axis, bit)
    return held[0]


def to_heads(pieces, blocks):
    rows, width = pieces[0].shape
    part = width // blocks
    packed = jnp.stack(
        [
            jnp.concatenate([piece[:, i * part : (i + 1) * part] for piece in pieces], axis=1)
            for i in range(blocks)
        ],
        axis=0,
    )
    moved = lax.all_to_all(packed, "blk", 0, 0)
    return moved.reshape(rows * blocks, part * len(pieces))


def swap_blocks(packed, blocks):
    length, columns = packed.shape
    return lax.all_to_all(packed.reshape(blocks, length // blocks, columns), "blk", 0, 0)


def side_by_side(moved, count):
    part = moved.shape[2] // count
    return [
        jnp.concatenate(
            [moved[j, :, i * part : (i + 1) * part] for j in range(moved.shape[0])], axis=1
        )
        for i in range(count)
    ]


def first_allowed(doc_ends, positions):
    first = jnp.zeros(positions.shape, jnp.int32)
    for number in range(doc_ends.shape[0]):
        end = doc_ends[number]
        first = jnp.maximum(first, jnp.where(end <= positions, end, 0))
    return first


def tile_probs(ends, packed, part, head, start, stop, factor):
    own = slice(head * HEAD, (head + 1) * HEAD)
    keys = packed[:stop, part + own.start : part + own.stop]
    scores = dot_rows(packed[start:stop, own], keys) * factor
    positions = start + lax.broadcasted_iota(jnp.int32, (stop - start, 1), 0)
    first = first_allowed(ends, positions)
    key_pos = lax.broadcasted_iota(jnp.int32, scores.shape, 1)
    allowed = (key_pos >= first) & (key_pos <= positions)
    scores = jnp.where(allowed, scores, NEGATIVE)
    weights = jnp.exp(scores - jnp.max(scores, axis=-1, keepdims=True))
    return weights / jnp.sum(weights, axis=-1, keepdims=True)


def attend_kernel(part, tile, factor, ends, packed, out):
    for head in range(part // HEAD):
        own = slice(head * HEAD, (head + 1) * HEAD)
        for start in range(0, packed.shape[0], tile):
            stop = start + tile
            probs = tile_probs(ends, packed, part, head, start, stop, factor)
            values = packed[:stop, 2 * part + own.start : 2 * part + own.stop]
            out[start:stop, own] = plain_dot(probs.astype(jnp.bfloat16), values).astype(out.dtype)


def attend_back_head(part, tile, factor, head, ends, packed, grads, out, key_sum, value_sum):
    length = packed.shape[0]
    own = slice(head * HEAD, (head + 1) * HEAD)
    key_own = slice(part + own.start, part + own.stop)
    value_own = slice(2 * part + own.start, 2 * part + own.stop)
    for start in reversed(range(0, length, tile)):
        stop = start + tile
        probs = tile_probs(ends, packed, part, head, start, stop, factor)
        grad = grads[start:stop, own]
        prob_grad = dot_rows(grad, packed[:stop, value_own])
        delta = jnp.sum(probs * prob_grad, axis=-1, keepdims=True)
        score_grad = (probs * (prob_grad - delta)).astype(jnp.bfloat16)
        query_grad = plain_dot(score_grad, packed[:stop, key_own]) * factor
        out[start:stop, own] = query_grad.astype(out.dtype)
        key_part = dot_cols(score_grad, packed[start:stop, own])
        value_part = dot_cols(probs.astype(jnp.bfloat16), grad)
        if stop == length:
            key_sum[:stop] = key_part
            value_sum[:stop] = value_part
        else:
            key_sum[:stop] += key_part
            value_sum[:stop] += value_part
    out[:, key_own] = (key_sum[...] * factor).astype(out.dtype)
    out[:, value_own] = value_sum[...].astype(out.dtype)


def attention_tile(length):
    return next(tile for tile in (512, 384, 256, 128, 64, 32, 16) if length % tile == 0)


def attention_call(kernel, doc_ends, arrays, columns, scratch, matmuls):
    length, width = arrays[0].shape
    part = width // 3
    tile = attention_tile(length)
    vmem = pl.BlockSpec(memory_space=pltpu.VMEM)
    return pl.pallas_call(
        functools.partial(kernel, part, tile, 1.0 / math.sqrt(HEAD)),
        out_shape=jax.ShapeDtypeStruct((length, columns), jnp.bfloat16),
        in_specs=[pl.BlockSpec(memory_space=pltpu.SMEM)] + [vmem] * len(arrays),
        out_specs=vmem,
        scratch_shapes=scratch,
        compiler_params=pltpu.CompilerParams(vmem_limit_bytes=48 * 1024 * 1024),
        cost_estimate=pl.CostEstimate(
            flops=2 * matmuls * length * length * part,
            bytes_accessed=10 * length * width,
            transcendentals=length * length * part // HEAD,
        ),
    )(doc_ends, *arrays)


def attend(doc_ends, packed):
    return attention_call(attend_kernel, doc_ends, [packed], packed.shape[1] // 3, [], 2)


def middle_kernel(
    fold, marks, tile, factor, ends, first_left, second_left, right_ref, attended_ref, cot_ref, gain_ref,
    weight_ref, packed_ref, mid, feed_ref, out_ref, resid_ref, gain_out, moved, result, *scratch
):
    count = len(fold[0][0])
    attended, cot, weight, packed, load_sem = scratch[:5]
    other, sent_grads, grads, out, key_sum, value_sum = scratch[5:11]
    heads_sem, ctx_sem, out_sem, strip_rows, strip_sem, ready = scratch[11:17]
    left_refs = (first_left, second_left)
    loads, turn, finish, partners = fold_engine(*fold, left_refs, right_ref, out_ref, scratch[17:])
    rows, features = mid.shape
    blocks, _, part = sent_grads.shape
    dp, blk, heads = (lax.axis_index(axis) for axis in MESH_AXES)

    def away(distance):
        at, bit = blk, 1
        while bit <= distance:
            if distance & bit:
                at = flipped(at, bit)
            bit *= 2
        return at

    mirror = (dp, blk, flipped(heads, 1))
    met = partners + [mirror]
    met += [(dp, away(d), heads) for d in range(1, blocks) if d & (d - 1)]
    loads = loads + [
        pltpu.make_async_copy(source, target, load_sem.at[number])
        for number, (source, target) in enumerate(
            [(attended_ref, attended), (cot_ref, cot), (weight_ref, weight), (packed_ref, packed)]
        )
    ]
    for load in loads:
        load.start()
    strip = strip_rows.shape[1]
    strips = features // strip
    units = right_ref.shape[2]

    def strip_copy(number):
        slot = lax.rem(number, 2)
        rows_of = pl.ds(pl.multiple_of(number * strip, strip), strip)
        return pltpu.make_async_copy(
            feed_ref.at[rows_of, pl.ds(2 * units, units)], strip_rows.at[slot], strip_sem.at[slot]
        )

    def strip_step(number):
        strip_copy(number).wait()

        @pl.when(number + 1 < strips)
        def _():
            strip_copy(number + 1).start()

        columns = pl.ds(pl.multiple_of(number * strip, strip), strip)
        product = dot_rows(right_ref[2], strip_rows[lax.rem(number, 2)])
        cot[:, columns] = product.astype(jnp.bfloat16)

    greet(met)

    def mirrored(source, number):
        return pltpu.make_async_remote_copy(
            src_ref=source,
            dst_ref=other,
            send_sem=heads_sem.at[0, number],
            recv_sem=heads_sem.at[1, number],
            device_id=mirror,
            device_id_type=MESH,
        )

    first, second = mirrored(mid, 0), mirrored(cot, 1)
    first.start()
    for load in loads:
        load.wait()

    def block(index):
        return pl.ds(pl.multiple_of(index * rows, rows), rows)

    def ctx_copy(distance, landing):
        return pltpu.make_async_remote_copy(
            src_ref=sent_grads.at[away(distance)],
            dst_ref=grads.at[block(landing)],
            send_sem=ctx_sem.at[0, distance],
            recv_sem=ctx_sem.at[1, distance],
            device_id=(dp, away(distance), heads),
            device_id_type=MESH,
        )

    def landing_of(kind, source):
        offset = kind * (part * blocks) + source * part
        return moved.at[:, pl.ds(pl.multiple_of(offset, part), part)]

    def out_copy(kind, distance, landing):
        return pltpu.make_async_remote_copy(
            src_ref=out.at[block(away(distance)), pl.ds(kind * part, part)],
            dst_ref=landing_of(kind, landing),
            send_sem=out_sem.at[0, kind, distance],
            recv_sem=out_sem.at[1, kind, distance],
            device_id=(dp, away(distance), heads),
            device_id_type=MESH,
        )

    step = rows // 3 if rows % 48 == 0 else rows
    starts = list(range(0, rows, step))

    def norm_back(start):
        if start == 0:
            first.wait()
        for start in (start,):
            own = slice(start, start + step)
            values = attended[own]
            mid_grad = pair_add(mid[own], other[own])
            scale = lax.rsqrt(jnp.mean(values * values, axis=-1, keepdims=True) + EPSILON)
            normed = values * scale
            scaled = mid_grad * gain_ref[...]
            inner = jnp.mean(scaled * normed, axis=-1, keepdims=True)
            total = cot[own].astype(jnp.float32) + scale * (scaled - normed * inner)
            resid_ref[own] = total
            gain_part = jnp.sum(mid_grad * normed, axis=0, keepdims=True)
            if start == 0:
                gain_out[...] = gain_part
            else:
                gain_out[...] += gain_part
            low = plain_dot(total.astype(jnp.bfloat16), weight[...]).astype(jnp.bfloat16)
            for number in range(blocks):
                sent_grads[number, own] = low[:, number * part : (number + 1) * part]
        if start != starts[-1]:
            return
        grads[block(blk)] = sent_grads[blk]
        for distance in range(1, blocks):
            ctx_copy(distance, blk).start()

    def one_head(head):
        attend_back_head(part, tile, factor, head, ends, packed, grads, out, key_sum, value_sum)

    def body(index, carry):
        turn(index)

        for number, start in enumerate(starts):

            @pl.when(index == marks[0] + number)
            def _(start=start):
                norm_back(start)

        done = marks[0] + len(starts) - 1

        @pl.when(index == done)
        def _():
            pl.semaphore_signal(ready, inc=1, device_id=mirror, device_id_type=MESH)
            strip_copy(jnp.int32(0)).start()

        @pl.when((index > done) & (index <= done + strips))
        def _():
            strip_step(index - done - 1)

        @pl.when(index == done + strips)
        def _():
            pl.semaphore_wait(ready, 1)
            second.start()

        @pl.when(index == marks[1])
        def _():
            for distance in range(1, blocks):
                ctx_copy(distance, away(distance)).wait_recv()
                ctx_copy(distance, blk).wait_send()

        for head in range(part // HEAD):

            @pl.when(index == marks[1] + head)
            def _(head=head):
                one_head(head)

        @pl.when(index == marks[1] + part // HEAD - 1)
        def _():
            for kind in range(3):
                offset = pl.multiple_of(kind * (part * blocks) + blk * part, part)
                moved[:, pl.ds(offset, part)] = out[block(blk), kind * part : (kind + 1) * part]

        for number in range(3 * (blocks - 1)):

            @pl.when(index == marks[1] + part // HEAD + 2 * number)
            def _(kind=number // (blocks - 1), distance=number % (blocks - 1) + 1):
                out_copy(kind, distance, blk).start()

        return carry

    lax.fori_loop(0, fold[2] + fold[6][-1], body, 0)
    finish()
    second.wait()
    for start in starts:
        own = slice(start, start + step)
        result[own] = (attended[own] + pair_add(cot[own], other[own])).astype(result.dtype)
    for kind in range(3):
        for distance in range(1, blocks):
            out_copy(kind, distance, away(distance)).wait_recv()
            out_copy(kind, distance, blk).wait_send()


def middle(lefts, rights, doc_ends, attended, cot, gain, weight, packed, mid, feed, call, marks, width=256, slots=10):
    each = rights.shape[2]
    sizes = [jax.ShapeDtypeStruct((1, each), jnp.bfloat16)] * 3
    fold, shape, scratch, cost = fold_layout(lefts, [sizes[:2], sizes[2:]], width, slots, 0)
    blocks = lax.axis_size("blk")
    rows, features = attended.shape
    length, columns = packed.shape
    part = columns // 3
    tile = 256 if length % 256 == 0 else attention_tile(length)
    turns = fold[2] + fold[6][-1]
    assert marks[0] + 3 + STRIPS < turns and marks[0] < marks[1] - 3
    assert marks[1] + part // HEAD + 2 * 3 * (blocks - 1) < turns
    vmem, anywhere = (pl.BlockSpec(memory_space=space) for space in (pltpu.VMEM, pl.ANY))
    low = jnp.bfloat16
    folded, resid, gain_grad, moved, result = pl.pallas_call(
        functools.partial(middle_kernel, fold, marks, tile, 1.0 / math.sqrt(HEAD)),
        out_shape=(
            shape,
            jax.ShapeDtypeStruct(attended.shape, jnp.float32),
            jax.ShapeDtypeStruct((1, features), jnp.float32),
            jax.ShapeDtypeStruct((rows, columns * blocks), low),
            jax.ShapeDtypeStruct((rows, features), low),
        ),
        in_specs=[
            pl.BlockSpec(memory_space=pltpu.SMEM),
            anywhere,
            anywhere,
            vmem,
            anywhere,
            anywhere,
            vmem,
            anywhere,
            anywhere,
            vmem,
            anywhere,
        ],
        out_specs=(vmem,) * 5,
        scratch_shapes=[
            pltpu.VMEM(attended.shape, jnp.float32),
            pltpu.VMEM(cot.shape, low),
            pltpu.VMEM(weight.shape, low),
            pltpu.VMEM(packed.shape, low),
            pltpu.SemaphoreType.DMA((4,)),
            pltpu.VMEM(cot.shape, low),
            pltpu.VMEM((blocks, rows, part), low),
            pltpu.VMEM((length, part), low),
            pltpu.VMEM((length, columns), low),
            pltpu.VMEM((length, HEAD), jnp.float32),
            pltpu.VMEM((length, HEAD), jnp.float32),
            pltpu.SemaphoreType.DMA((2, 2)),
            pltpu.SemaphoreType.DMA((2, blocks)),
            pltpu.SemaphoreType.DMA((2, 3, blocks)),
            pltpu.VMEM((2, features // STRIPS, each), low),
            pltpu.SemaphoreType.DMA((2,)),
            pltpu.SemaphoreType.REGULAR,
            *scratch,
        ],
        compiler_params=remote_params(call),
        cost_estimate=cost,
    )(doc_ends, *lefts, rights, attended, cot, gain[None], weight, packed, mid, feed)
    shares = [folded[:, number * each : (number + 1) * each] for number in range(3)]
    return shares, resid, gain_grad[0], moved, result


def last_kernel(
    fold, marks, first_left, second_left, third_left, right_ref, normed_part, memory_part, hidden_ref,
    memory_ref, resid_ref, gains_ref, mid_gain_ref, out_ref, hidden_grad, memory_grad, gain_out, *scratch
):
    steps = fold[0][0]
    count = len(steps)
    normed_other, memory_other, hidden, memory, resid = scratch[:5]
    load_sem, heads_sem, gain_sem, gain_held = scratch[5:9]
    gain_got = scratch[9 : 9 + count]
    left_refs = (first_left, second_left, third_left)
    loads, turn, finish, partners = fold_engine(
        *fold, left_refs, right_ref, out_ref, scratch[9 + count :]
    )
    rows, features = normed_part.shape
    dp, blk, heads = (lax.axis_index(axis) for axis in MESH_AXES)
    mirror = (dp, blk, flipped(heads, 1))
    loads = loads + [
        pltpu.make_async_copy(source, target, load_sem.at[number])
        for number, (source, target) in enumerate(
            [(hidden_ref, hidden), (memory_ref, memory), (resid_ref, resid)]
        )
    ]
    for load in loads:
        load.start()
    greet(partners + [mirror])
    mirrored = [
        pltpu.make_async_remote_copy(
            src_ref=source,
            dst_ref=target,
            send_sem=heads_sem.at[0, number],
            recv_sem=heads_sem.at[1, number],
            device_id=mirror,
            device_id_type=MESH,
        )
        for number, (source, target) in enumerate(
            [(normed_part, normed_other), (memory_part, memory_other)]
        )
    ]
    for copy in mirrored:
        copy.start()
    for load in loads:
        load.wait()
    offsets, part = fold_order(features, steps)

    def keep_gain(number, gain_grad):
        for place, offset in enumerate(offsets):
            columns = pl.ds(pl.multiple_of(offset, part), part)
            gain_held[place, number : number + 1] = gain_grad[:, columns]

    def norm_back(number):
        mirrored[number].wait()
        own, other = ((normed_part, normed_other), (memory_part, memory_other))[number]
        source, target = ((hidden, hidden_grad), (memory, memory_grad))[number]
        step = rows // 3 if rows % 48 == 0 else rows
        gain_total = None
        for start in range(0, rows, step):
            here = slice(start, start + step)
            values = source[here].astype(jnp.float32)
            grad = pair_add(own[here], other[here])
            scale = lax.rsqrt(jnp.mean(values * values, axis=-1, keepdims=True) + EPSILON)
            normed = values * scale
            scaled = grad * gains_ref[number : number + 1]
            inner = jnp.mean(scaled * normed, axis=-1, keepdims=True)
            total = scale * (scaled - normed * inner)
            target[here] = total + resid[here] if number == 0 else total
            gain_part = jnp.sum(grad * normed, axis=0, keepdims=True)
            gain_total = gain_part if gain_total is None else gain_total + gain_part
        gain_sum[...] = gain_total
        keep_gain(number, gain_sum)

    gain_sum = scratch[-1]

    def gain_copy(step):
        half = (1 << count) >> (step + 1)
        return pltpu.make_async_remote_copy(
            src_ref=gain_held.at[pl.ds(half, half)],
            dst_ref=gain_got[step],
            send_sem=gain_sem.at[0, step],
            recv_sem=gain_sem.at[1, step],
            device_id=partners[step],
            device_id_type=MESH,
        )

    def gain_step(step):
        if step > 0:
            gain_copy(step - 1).wait()
            half = (1 << count) >> step
            gain_held[:half] += gain_got[step - 1][...]
        if step < count:
            gain_copy(step).start()

    def body(index, carry):
        turn(index)

        @pl.when(index == marks[0])
        def _():
            gain_held[...] = jnp.zeros_like(gain_held)
            keep_gain(2, mid_gain_ref)
            norm_back(0)

        @pl.when(index == marks[1])
        def _():
            norm_back(1)

        for step in range(count):

            @pl.when(index == marks[1] + step)
            def _(step=step):
                gain_step(step)

        return carry

    lax.fori_loop(0, fold[2] + fold[6][-1], body, 0)
    gain_step(count)
    gain_out[...] = gain_held[0]
    finish()


def last(groups, normed_part, memory_part, hidden, memory, resid, gains, mid_gain_grad, call, marks, width=256, slots=12):
    fold, lefts, rights, shape, scratch, cost = fold_setting(groups, width, slots, 6)
    count = len(fold[0][0])
    marks = tuple(min(mark, fold[2] + fold[6][-1] - count) for mark in marks)
    rows, features = normed_part.shape
    part = features >> count
    vmem, anywhere = (pl.BlockSpec(memory_space=space) for space in (pltpu.VMEM, pl.ANY))
    folded, hidden_grad, memory_grad, gain_grads = pl.pallas_call(
        functools.partial(last_kernel, fold, marks),
        out_shape=(
            shape,
            jax.ShapeDtypeStruct(hidden.shape, jnp.float32),
            jax.ShapeDtypeStruct(hidden.shape, jnp.float32),
            jax.ShapeDtypeStruct((8, part), jnp.float32),
        ),
        in_specs=[anywhere] * 3 + [vmem] * 3 + [anywhere] * 3 + [vmem] * 2,
        out_specs=(vmem,) * 4,
        scratch_shapes=[
            pltpu.VMEM(hidden.shape, jnp.bfloat16),
            pltpu.VMEM(hidden.shape, jnp.bfloat16),
            pltpu.VMEM(hidden.shape, jnp.bfloat16),
            pltpu.VMEM(hidden.shape, jnp.bfloat16),
            pltpu.VMEM(hidden.shape, jnp.float32),
            pltpu.SemaphoreType.DMA((3,)),
            pltpu.SemaphoreType.DMA((2, 2)),
            pltpu.SemaphoreType.DMA((2, count)),
            pltpu.VMEM((1 << count, 8, part), jnp.float32),
            *[pltpu.VMEM(((1 << count) >> (step + 1), 8, part), jnp.float32) for step in range(count)],
            *scratch,
            pltpu.VMEM((1, features), jnp.float32),
        ],
        compiler_params=remote_params(call),
        cost_estimate=cost,
    )(*lefts, rights, normed_part, memory_part, hidden, memory, resid, gains, mid_gain_grad[None])
    return unstacked(groups, folded), hidden_grad, memory_grad, gain_grads


def feed_kernel(mid_ref, cot_ref, gate_ref, up_ref, down_ref, out_ref, grad_ref, total):
    gate = plain_dot(mid_ref[...], gate_ref[...])
    upward = plain_dot(mid_ref[...], up_ref[...])
    act_grad = plain_dot(cot_ref[...], down_ref[...])
    sigma = jax.nn.sigmoid(gate)
    silu_gate = gate * sigma
    gate_grad = act_grad * upward * sigma * (1.0 + gate * (1.0 - sigma))
    gate_low = gate_grad.astype(jnp.bfloat16)
    up_low = (act_grad * silu_gate).astype(jnp.bfloat16)
    out_ref[0] = gate_low
    out_ref[1] = up_low
    out_ref[2] = (silu_gate * upward).astype(jnp.bfloat16)
    step = pl.program_id(0)

    @pl.when(step == 0)
    def _():
        total[...] = jnp.zeros_like(total)

    total[...] += dot_rows(gate_low, gate_ref[...]) + dot_rows(up_low, up_ref[...])

    @pl.when(step == pl.num_programs(0) - 1)
    def _():
        grad_ref[...] = total[...].astype(jnp.bfloat16)


def feed(mid, cot, full, width=256):
    rows, features = mid.shape
    units = full.shape[1] // 3
    steps = units // width
    whole = pl.BlockSpec((rows, features), lambda i: (0, 0))
    return pl.pallas_call(
        feed_kernel,
        grid=(steps,),
        out_shape=(
            jax.ShapeDtypeStruct((3, rows, units), jnp.bfloat16),
            jax.ShapeDtypeStruct((rows, features), jnp.bfloat16),
        ),
        in_specs=[whole, whole]
        + [
            pl.BlockSpec((features, width), lambda i, number=number: (0, number * steps + i))
            for number in range(3)
        ],
        out_specs=(pl.BlockSpec((3, rows, width), lambda i: (0, 0, i)), whole),
        scratch_shapes=[pltpu.VMEM((rows, features), jnp.float32)],
        compiler_params=pltpu.CompilerParams(vmem_limit_bytes=40 * 1024 * 1024),
        cost_estimate=pl.CostEstimate(
            flops=10 * rows * features * units,
            bytes_accessed=6 * features * units,
            transcendentals=rows * units,
        ),
    )(mid, cot, full, full, full)


def by_head(array):
    return array.reshape(array.shape[0], -1, HEAD).transpose(1, 0, 2)


def from_heads(array):
    return array.transpose(1, 0, 2).reshape(array.shape[1], -1).astype(jnp.bfloat16)


def plain_probs(doc_ends, query_pos, query, key):
    key_pos = jnp.arange(key.shape[0], dtype=jnp.int32)
    first = first_allowed(doc_ends, query_pos)
    allowed = (key_pos[None, :] >= first[:, None]) & (key_pos[None, :] <= query_pos[:, None])
    scores = dot_rows(query, key) * (1.0 / math.sqrt(HEAD))
    return jax.nn.softmax(jnp.where(allowed, scores, NEGATIVE), axis=-1)


def plain_attend(doc_ends, query_pos, queries, keys, values):
    def one(arrays):
        query, key, value = arrays
        probs = plain_probs(doc_ends, query_pos, query, key)
        return plain_dot(probs.astype(jnp.bfloat16), value)

    return from_heads(lax.map(one, (by_head(queries), by_head(keys), by_head(values))))


def plain_attend_back(doc_ends, query_pos, queries, keys, values, grads):
    factor = 1.0 / math.sqrt(HEAD)

    def one(arrays):
        query, key, value, grad = arrays
        probs = plain_probs(doc_ends, query_pos, query, key)
        prob_grad = dot_rows(grad, value)
        delta = jnp.sum(probs * prob_grad, axis=-1, keepdims=True)
        score_grad = (probs * (prob_grad - delta)).astype(jnp.bfloat16)
        return (
            plain_dot(score_grad, key) * factor,
            dot_cols(score_grad, query) * factor,
            dot_cols(probs.astype(jnp.bfloat16), grad),
        )

    arrays = tuple(by_head(array) for array in (queries, keys, values, grads))
    return tuple(from_heads(grad) for grad in lax.map(one, arrays))


def local(
    hidden_in,
    memory,
    lengths,
    query_weight,
    key_weight,
    value_weight,
    output_weight,
    gate_weight,
    up_weight,
    down_weight,
    attention_gain,
    memory_gain,
    feedforward_gain,
    cotangent,
):
    rows, features = hidden_in.shape
    blocks = lax.axis_size("blk")
    width = query_weight.shape[1]
    hidden_units = gate_weight.shape[1]
    heads_local = width // HEAD
    spread = heads_local % blocks == 0 and lax.axis_size("heads") == 2
    doc_ends = jnp.cumsum(lengths[0], dtype=jnp.int32)

    gains = jnp.stack([attention_gain, memory_gain, feedforward_gain], axis=1)
    gains = jnp.pad(gains, ((0, 0), (0, LANES - gains.shape[1])))
    attn_mine = jnp.concatenate(
        [query_weight, key_weight, value_weight, output_weight, gains], axis=1
    )
    attn_full = lax.all_gather(attn_mine, ("dp", "blk"), axis=0, tiled=True)
    padded = -(-hidden_units // (2 * LANES)) * (2 * LANES)
    ffn_mine = jnp.concatenate(
        [
            jnp.pad(weight, ((0, 0), (0, padded - hidden_units)))
            for weight in (gate_weight, up_weight, down_weight)
        ],
        axis=1,
    )
    ffn_mine, attn_full = together(ffn_mine, attn_full)
    ffn_full = lax.all_gather(ffn_mine, ("dp", "blk"), axis=0, tiled=True)

    full_query = attn_full[:, :width]
    full_key = attn_full[:, width : 2 * width]
    full_value = attn_full[:, 2 * width : 3 * width]
    full_output = attn_full[:, 3 * width : 4 * width]
    full_gains = attn_full[:, 4 * width : 4 * width + 3].astype(jnp.float32).T
    input_gain, source_gain, mid_gain = full_gains[0], full_gains[1], full_gains[2]

    hidden_float = hidden_in.astype(jnp.float32)
    memory_float = memory.astype(jnp.float32)
    memory_low = rms_scale(memory_float, source_gain).astype(jnp.bfloat16)
    normed_low = rms_scale(hidden_float, input_gain).astype(jnp.bfloat16)
    key_low = plain_dot(memory_low, full_key).astype(jnp.bfloat16)
    value_low = plain_dot(memory_low, full_value).astype(jnp.bfloat16)
    query_low = plain_dot(normed_low, full_query).astype(jnp.bfloat16)

    if spread:
        packed = to_heads([query_low, key_low, value_low], blocks)
        context_low = side_by_side(swap_blocks(attend(doc_ends, packed), blocks), 1)[0]
    else:
        query_pos = lax.axis_index("blk") * rows + jnp.arange(rows, dtype=jnp.int32)
        key_all = lax.all_gather(key_low, "blk", axis=0, tiled=True)
        value_all = lax.all_gather(value_low, "blk", axis=0, tiled=True)
        context_low = plain_attend(doc_ends, query_pos, query_low, key_all, value_all)

    attended = hidden_float + pair_sum(dot_rows(context_low, full_output))
    attended, cot_turned, normed_turned, memory_turned = together(
        attended, cotangent.T, normed_low.T, memory_low.T
    )
    mid_low = rms_scale(attended, mid_gain).astype(jnp.bfloat16)

    rights, mid_part = feed(mid_low, cotangent, ffn_full)
    full_down = ffn_full[:, 2 * padded :]
    if spread:
        shares, attended_grad, mid_gain_grad, moved, output = middle(
            (mid_low.T, cot_turned),
            rights,
            doc_ends,
            attended,
            cotangent,
            mid_gain,
            full_output,
            packed,
            mid_part,
            ffn_full,
            0,
            MARKS,
        )
        resid_low = attended_grad.astype(jnp.bfloat16)
        query_grad_low, key_grad_low, value_grad_low = (
            moved[:, i * width : (i + 1) * width] for i in range(3)
        )
    else:
        gate_grad_low, up_grad_low, act_low = rights[0], rights[1], rights[2]
        shares = fold_products(
            [(mid_low.T, [gate_grad_low, up_grad_low]), (cot_turned, [act_low])], 0
        )
        shares = [*shares[0], *shares[1]]
        output = (attended + pair_sum(dot_rows(act_low, full_down))).astype(jnp.bfloat16)
        mid_grad = pair_sum(mid_part)
        attended_norm_grad, mid_gain_grad = jax.vjp(rms_scale, attended, mid_gain)[1](mid_grad)
        attended_grad = cotangent.astype(jnp.float32) + attended_norm_grad
        resid_low = attended_grad.astype(jnp.bfloat16)
        context_grad_low = plain_dot(resid_low, full_output).astype(jnp.bfloat16)
        query_grad_low, key_grad, value_grad = plain_attend_back(
            doc_ends, query_pos, query_low, key_all, value_all, context_grad_low
        )
        moved = lax.psum_scatter(
            jnp.concatenate([key_grad, value_grad], axis=1), "blk", scatter_dimension=0, tiled=True
        )
        key_grad_low, value_grad_low = moved[:, :width], moved[:, width:]
    gate_share, up_share, down_share = shares
    normed_part = dot_rows(query_grad_low, full_query).astype(jnp.bfloat16)
    memory_part = (
        dot_rows(key_grad_low, full_key) + dot_rows(value_grad_low, full_value)
    ).astype(jnp.bfloat16)
    if spread:
        right_sets = ([context_low], [moved[:, :width]], [moved[:, width:]])
    else:
        right_sets = ([context_low], [query_grad_low], [key_grad_low, value_grad_low])
    products = list(zip((resid_low.T, normed_turned, memory_turned), right_sets))
    if spread:
        shares, hidden_grad, memory_grad, gain_shares = last(
            products,
            normed_part,
            memory_part,
            hidden_in,
            memory,
            attended_grad,
            jnp.stack([input_gain, source_gain], axis=0),
            mid_gain_grad,
            1,
            LAST_MARKS,
        )
    else:
        shares = fold_products(products, 1)
        normed_grad = pair_sum(normed_part)
        memory_in_grad = pair_sum(memory_part)
        hidden_norm_grad, input_gain_grad = jax.vjp(rms_scale, hidden_float, input_gain)[1](
            normed_grad
        )
        memory_grad, source_gain_grad = jax.vjp(rms_scale, memory_float, source_gain)[1](
            memory_in_grad
        )
        hidden_grad = attended_grad + hidden_norm_grad
        gain_shares = fold_vector(
            jnp.stack([input_gain_grad, source_gain_grad, mid_gain_grad], axis=0)
        )
    (output_share,), (query_share,), both = shares
    both = jnp.concatenate(both, axis=1)
    key_share, value_share = both[:, :width], both[:, width:]
    gate_share, up_share, down_share = (
        share[:, :hidden_units] for share in (gate_share, up_share, down_share)
    )
    return (
        output,
        hidden_grad,
        memory_grad,
        query_share,
        key_share,
        value_share,
        output_share,
        gate_share,
        up_share,
        down_share,
        gain_shares[0],
        gain_shares[1],
        gain_shares[2],
    )


def solution(mesh):
    tokens = P(("dp", "blk"), None)
    weight = P(("dp", "blk"), "heads")
    gain = P(("dp", "blk"))
    return jax.shard_map(
        local,
        mesh=mesh,
        in_specs=(tokens, tokens, P("dp", None)) + (weight,) * 7 + (gain,) * 3 + (tokens,),
        out_specs=(tokens,) * 3 + (weight,) * 7 + (gain,) * 3,
        check_vma=False,
    )
```
